32 devices in a mesh: replica: 4 (over y, x), fsdp: 8 (over z, core).
Axes of the slice: x: 2, y: 2, z: 4, core: 2. Of those that a mesh axis runs over, the one named last changes fastest.
Arguments:
- tokens: bfloat16 [4, 8192, 4096], P('replica', 'fsdp'), may hold values from -6 to 6
- norm_gain: float32 [4096], replicated, may hold values from 0.25 to 1.75
- value_weight: bfloat16 [4, 4096, 512], P('replica', 'fsdp'), may hold values from -0.09375 to 0.09375
- output_weight: bfloat16 [4, 4096, 512], P('replica', 'fsdp'), may hold values from -0.25 to 0.25
- out_cotangent: bfloat16 [4, 8192, 4096], P('replica', 'fsdp'), may hold values from -0.21875 to 0.21875
- base_params: bfloat16 [65536, 128], P('fsdp'), may hold values from -6 to 6
- outer_momentum: float32 [65536, 128], P('fsdp'), may hold values from -4 to 4
- delta_values: bfloat16 [4, 65536, 128], P('replica', 'fsdp'), may hold values from -8 to 8
- delta_exponents: int32 [4, 65536], P('replica', 'fsdp'), may hold values from -3 to 1
Outputs:
- value_grad: float32 [4, 4096, 512], P('replica', 'fsdp')
- output_grad: float32 [4, 4096, 512], P('replica', 'fsdp')
- new_base: bfloat16 [65536, 128], P('fsdp')
- new_momentum: float32 [65536, 128], P('fsdp')
The draws below stay inside these ranges and needn't reach their ends.
All inputs are finite; a program needn't handle non-finite values.
Results may differ from the reference program's by a relative error of at most 0.015.
Values may be sent and summed in bfloat16 or wider, within the bound.
No kernel may reach another device: no remote copies, remote signals or barrier semaphores. Data moves between devices by JAX's collectives and lax.ppermute only.
A program may use at most 128 MiB of HBM per device.

```python
import jax
import jax.numpy as jnp
from jax import lax

D = 4096
KV = 512
TOK_DEV = 1024
FRAG_ROWS = 65536
TOKENS = 8192
N_REPLICA = 4
N_FSDP = 8


def place_ends(drawn, rng, least, top_value):
    longest = drawn.shape.index(max(drawn.shape))
    spots = []
    for shift in (0, 1):
        where = [jax.random.randint(jax.random.fold_in(rng, axis), (), 0, length) for axis, length in enumerate(drawn.shape)]
        where[longest] = (where[longest] + shift) % drawn.shape[longest]
        spots.append(tuple(where))
    return drawn.at[spots[0]].set(least).at[spots[1]].set(top_value)


def raised(result, stream_key, source, target, parts, factor):
    owner, partner = [(jnp.arange(result.shape[axis_at]) // (result.shape[axis_at] // parts)).reshape([-1 if axis == axis_at else 1 for axis in range(result.ndim)]) for axis_at in (source, target)]
    chosen = jax.random.permutation(stream_key, parts)[partner]
    strong = (owner == chosen) | (owner == (partner + parts // 2) % parts)
    return jnp.where(strong, factor * result, result)


def shard_levels(key, dims, shards, smallest, largest):
    def one(axis_at, blocks):
        steps = jax.random.uniform(jax.random.fold_in(jax.random.fold_in(key, 6), axis_at), (blocks,), jnp.float32, smallest / len(shards), largest / len(shards))
        return jnp.repeat(jnp.exp(steps), dims[axis_at] // blocks).reshape((-1,) + (1,) * (len(dims) - axis_at - 1))

    level = one(*shards[0])
    for cut in shards[1:]:
        level = level * one(*cut)
    return level


def noise(stream_key, dims, spread, limit, pieces=(), held_as=jnp.bfloat16):
    factor_of = shard_levels(stream_key, dims, pieces, -0.22, 0.18) if pieces else 1.0
    values = jax.random.normal(stream_key, dims, jnp.float32) * spread * factor_of
    return jnp.minimum(jnp.maximum(values, -limit), limit).astype(held_as)


def heavy_noise(rng, shape, scale, bound, cuts, heavy, dtype=jnp.bfloat16):
    drawn = scale * jax.random.normal(rng, shape, jnp.float32)
    if cuts:
        drawn = drawn * shard_levels(rng, shape, cuts, -0.22, 0.18)
    return jnp.clip(raised(drawn, jax.random.fold_in(rng, 3), *heavy), -bound, bound).astype(dtype)


def setup_inputs(seed: int = 0) -> dict:
    keys = jax.random.split(jax.random.key(seed), 10)
    tokens = noise(keys[0], (N_REPLICA, TOKENS, D), 1.0, 6.0, ((0, 4), (1, 8)))
    norm_gain = jnp.clip(1.0 + 0.15 * jax.random.normal(keys[1], (D,), jnp.float32), 0.25, 1.75)
    value_weight = noise(keys[2], (N_REPLICA, D, KV), D ** -0.5, 0.09375, ((0, 4), (1, 8)))
    output_weight = noise(keys[3], (N_REPLICA, D, KV), KV ** -0.5, 0.25, ((0, 4), (1, 8)))
    out_cotangent = heavy_noise(keys[4], (N_REPLICA, TOKENS, D), (TOKENS ** -0.5), 0.21875, ((0, 4), (1, 8)), (1, 2, 8, 2.0))
    base_params = noise(keys[5], (FRAG_ROWS, 128), 1.0, 6.0, ((0, 8),))
    outer_momentum = noise(keys[6], (FRAG_ROWS, 128), 0.5, 4.0, ((0, 8),), jnp.float32)
    delta_values = noise(keys[7], (N_REPLICA, FRAG_ROWS, 128), 1.0, 8.0, ((0, 4), (1, 8)))
    delta_exponents = place_ends(jax.random.randint(keys[8], (N_REPLICA, FRAG_ROWS), -3, 2), jax.random.fold_in(keys[8], 1), -3, 1).astype(jnp.int32)
    return {"tokens": tokens, "norm_gain": norm_gain, "value_weight": value_weight, "output_weight": output_weight, "out_cotangent": out_cotangent, "base_params": base_params, "outer_momentum": outer_momentum, "delta_values": delta_values, "delta_exponents": delta_exponents}


def group_terms(left, right):
    left_groups = left.reshape(N_FSDP, TOK_DEV, left.shape[1])
    right_groups = right.reshape(N_FSDP, TOK_DEV, right.shape[1])

    def one_group(pair):
        term = lax.dot_general(pair[0], pair[1], (((0,), (0,)), ((), ())), preferred_element_type=jnp.float32)
        return term.astype(jnp.bfloat16).astype(jnp.float32)
    terms = lax.map(one_group, (left_groups, right_groups))
    return lax.optimization_barrier(jnp.sum(terms, axis=0))

def replica_grads(tokens_one, gain, value_w, output_w, cotangent):
    xf = tokens_one.astype(jnp.float32)
    scale = lax.rsqrt(lax.optimization_barrier(jnp.mean(xf * xf, axis=1, keepdims=True)) + 1e-05)
    normed = (xf * scale * gain).astype(jnp.bfloat16)
    values = jnp.dot(normed, value_w, preferred_element_type=jnp.float32).astype(jnp.bfloat16)
    value_cot = jnp.dot(cotangent, output_w, preferred_element_type=jnp.float32).astype(jnp.bfloat16)
    output_grad = group_terms(cotangent, values)
    value_grad = group_terms(normed, value_cot)
    return (value_grad, output_grad)

def reference(tokens, norm_gain, value_weight, output_weight, out_cotangent, base_params, outer_momentum, delta_values, delta_exponents):
    value_list = []
    output_list = []
    for index in range(N_REPLICA):
        value_grad, output_grad = replica_grads(tokens[index], norm_gain, value_weight[index], output_weight[index], out_cotangent[index])
        value_list.append(value_grad)
        output_list.append(output_grad)
    scaled = delta_values.astype(jnp.float32) * jnp.exp2(delta_exponents.astype(jnp.float32))[:, :, None]
    delta = lax.optimization_barrier(jnp.sum(scaled, axis=0)) * (1.0 / N_REPLICA)
    new_momentum = 0.9 * outer_momentum + delta
    new_base = (base_params.astype(jnp.float32) - 0.7 * (delta + 0.9 * new_momentum)).astype(jnp.bfloat16)
    return (jnp.stack(value_list), jnp.stack(output_list), new_base, new_momentum)
```

```python
import jax
import jax.numpy as jnp
from jax import lax
from jax.experimental import pallas as pl
from jax.experimental.pallas import tpu as pltpu
from jax.sharding import PartitionSpec as P

CHUNKS = 2
ROW_TILE = 128


def nesterov(delta, base_part, momentum_part):
    momentum_next = 0.9 * momentum_part + delta
    base_next = (base_part.astype(jnp.float32) - 0.7 * (delta + 0.9 * momentum_next)).astype(
        jnp.bfloat16
    )
    return (base_next, momentum_next)


def prepare_kernel(blocks, width, order_ref, tokens_ref, cot_ref, gain_ref, n0, n1, c0, c1):
    xf = tokens_ref[...].astype(jnp.float32)
    scale = lax.rsqrt(jnp.mean(xf * xf, axis=1, keepdims=True) + 1e-05)
    for place in range(blocks):
        for core, (n_out, c_out) in enumerate(((n0, c0), (n1, c1))):
            start = pl.multiple_of(order_ref[core * blocks + place] * width, width)
            cols = pl.ds(start, width)
            to = slice(place * width, (place + 1) * width)
            part = tokens_ref[:, cols].astype(jnp.float32)
            n_out[:, to] = (part * scale * gain_ref[:, cols]).astype(jnp.bfloat16)
            c_out[:, to] = cot_ref[:, cols]


def prepare(tokens, cotangent, gain, order):
    rows, model = tokens.shape
    blocks = order.shape[0] // 2
    half = model // 2

    def kernel(*refs):
        prepare_kernel(blocks, half // blocks, *refs)

    wide = pl.BlockSpec((ROW_TILE, model), lambda i, order_ref: (i, 0))
    out = pl.BlockSpec((ROW_TILE, half), lambda i, order_ref: (i, 0))
    return pl.pallas_call(
        kernel,
        grid_spec=pltpu.PrefetchScalarGridSpec(
            num_scalar_prefetch=1,
            grid=(rows // ROW_TILE,),
            in_specs=[wide, wide, pl.BlockSpec((1, model), lambda i, order_ref: (0, 0))],
            out_specs=[out] * 4,
        ),
        out_shape=[jax.ShapeDtypeStruct((rows, half), jnp.bfloat16)] * 4,
        compiler_params=pltpu.CompilerParams(vmem_limit_bytes=32 * 1024 * 1024),
        cost_estimate=pl.CostEstimate(
            flops=6 * rows * model, bytes_accessed=8 * rows * model, transcendentals=rows
        ),
    )(order, tokens, cotangent, gain[None])


def tie(value, after):
    return lax.optimization_barrier((value, after))[0]


def line_perm(chips, senders, shift):
    return [(2 * z + c, 2 * (z + shift) + c) for z in senders for c in (0, 1)]


def gather_line(own, chips, after):
    right, left = [own], [own]
    for step in range(1, chips):
        to_right, to_left = right[-1], left[-1]
        if step == 1 and after is not None:
            to_right, to_left = tie(to_right, after), tie(to_left, after)
        right.append(
            lax.ppermute(to_right, "fsdp", line_perm(chips, range(step - 1, chips - 1), 1))
        )
        left.append(
            lax.ppermute(to_left, "fsdp", line_perm(chips, range(1, chips - step + 1), -1))
        )
    places = [own] + [right[s] + left[chips - s] for s in range(1, chips)]
    return (jnp.concatenate(places, axis=0), right[chips - 2])


def scatter_line(keep, other, chips, width):
    def term(place):
        cols = slice(place * width, (place + 1) * width)
        return keep[:, cols].astype(jnp.float32) + other[:, cols].astype(jnp.float32)

    right = left = None
    for step in range(1, chips):
        to_right, to_left = term(step), term(chips - step)
        if right is not None:
            to_right, to_left = to_right + right, to_left + left
        right = lax.ppermute(
            to_right.astype(jnp.bfloat16), "fsdp", line_perm(chips, range(0, step), 1)
        ).astype(jnp.float32)
        left = lax.ppermute(
            to_left.astype(jnp.bfloat16), "fsdp", line_perm(chips, range(chips - step, chips), -1)
        ).astype(jnp.float32)
    return term(0) + right + left


def per_device(
    tokens,
    norm_gain,
    value_weight,
    output_weight,
    out_cotangent,
    base_params,
    outer_momentum,
    delta_values,
    delta_exponents,
):
    replicas = lax.axis_size("replica")
    devices = lax.axis_size("fsdp")
    chips = devices // 2
    me = lax.axis_index("fsdp")
    chip, core = me // 2, me % 2
    swap = [(i, i ^ 1) for i in range(devices)]
    width = tokens.shape[2] // devices

    scaled = (
        delta_values[0].astype(jnp.float32)
        * jnp.exp2(delta_exponents[0].astype(jnp.float32))[:, None]
    )
    delta = lax.psum(scaled.astype(jnp.bfloat16), "replica").astype(jnp.float32) * (1.0 / replicas)

    source = (chip - jnp.arange(chips, dtype=jnp.int32) + chips) % chips
    order = jnp.concatenate([2 * source + core, 2 * source + 1 - core]).astype(jnp.int32)
    normed0, normed1, cot0, cot1 = prepare(tokens[0], out_cotangent[0], norm_gain, order)

    features = value_weight.shape[2]
    piece = features // CHUNKS
    after = None
    sums = {}
    for name, weight, (in0, in1), (out0, out1) in (
        ("output", value_weight[0], (normed0, normed1), (cot0, cot1)),
        ("value", output_weight[0], (cot0, cot1), (normed0, normed1)),
    ):
        parts = []
        for chunk in range(CHUNKS):
            own = weight[:, chunk * piece : (chunk + 1) * piece]
            w0, after = gather_line(own, chips, after)
            w1 = lax.ppermute(w0, "fsdp", swap)
            mid = (
                jnp.dot(in0, w0, preferred_element_type=jnp.float32)
                + jnp.dot(in1, w1, preferred_element_type=jnp.float32)
            ).astype(jnp.bfloat16)

            def grad(out):
                return lax.dot_general(
                    mid, out, (((0,), (0,)), ((), ())), preferred_element_type=jnp.float32
                ).astype(jnp.bfloat16)

            other = lax.ppermute(grad(out1), "fsdp", swap)
            keep = grad(out0)
            parts.append(scatter_line(keep, other, chips, width).T)
        sums[name] = jnp.concatenate(parts, axis=1)

    new_base, new_momentum = nesterov(delta, base_params, outer_momentum)
    return (sums["value"][None], sums["output"][None], new_base, new_momentum)


def solution(mesh):
    return jax.shard_map(
        per_device,
        mesh=mesh,
        in_specs=(
            P("replica", "fsdp", None),
            P(),
            P("replica", "fsdp", None),
            P("replica", "fsdp", None),
            P("replica", "fsdp", None),
            P("fsdp", None),
            P("fsdp", None),
            P("replica", "fsdp", None),
            P("replica", "fsdp"),
        ),
        out_specs=(
            P("replica", "fsdp", None),
            P("replica", "fsdp", None),
            P("fsdp", None),
            P("fsdp", None),
        ),
        check_vma=False,
    )
```

```python
import jax
import jax.numpy as jnp
from jax import lax
from jax.experimental import pallas as pl
from jax.experimental.pallas import tpu as pltpu
from jax.sharding import PartitionSpec as P

STREAMS = 2
ROW_TILE = 128
MIB = 1024 * 1024


def nesterov(delta, base_part, momentum_part):
    momentum_next = 0.9 * momentum_part + delta
    base_next = (base_part.astype(jnp.float32) - 0.7 * (delta + 0.9 * momentum_next)).astype(
        jnp.bfloat16
    )
    return (base_next, momentum_next)


def move_perm(chips, active):
    pairs = []
    for z in range(chips):
        if z < chips - 1 and active(z):
            pairs.append((2 * z, 2 * z + 2))
        if z > 0 and active(chips - 1 - z):
            pairs.append((2 * z + 1, 2 * z - 1))
    return pairs


def call(kernel, place, grid, in_specs, out_specs, out_shape, flops, moved, scratch=(), vmem=32):
    return pl.pallas_call(
        kernel,
        grid_spec=pltpu.PrefetchScalarGridSpec(
            num_scalar_prefetch=1,
            grid=grid,
            in_specs=in_specs,
            out_specs=out_specs,
            scratch_shapes=scratch,
        ),
        out_shape=out_shape,
        compiler_params=pltpu.CompilerParams(vmem_limit_bytes=vmem * MIB),
        cost_estimate=pl.CostEstimate(flops=flops, bytes_accessed=moved, transcendentals=0),
    )


def normalise(tokens, gain):
    rows, model = tokens.shape

    def kernel(tokens_ref, gain_ref, out_ref):
        xf = tokens_ref[...].astype(jnp.float32)
        scale = lax.rsqrt(jnp.mean(xf * xf, axis=1, keepdims=True) + 1e-05)
        out_ref[...] = (xf * scale * gain_ref[...]).astype(jnp.bfloat16)

    tile = pl.BlockSpec((ROW_TILE, model), lambda i: (i, 0))
    return pl.pallas_call(
        kernel,
        grid=(rows // ROW_TILE,),
        in_specs=[tile, pl.BlockSpec((1, model), lambda i: (0, 0))],
        out_specs=tile,
        out_shape=jax.ShapeDtypeStruct((rows, model), jnp.bfloat16),
        compiler_params=pltpu.CompilerParams(vmem_limit_bytes=32 * MIB),
        cost_estimate=pl.CostEstimate(
            flops=6 * rows * model, bytes_accessed=4 * rows * model, transcendentals=rows
        ),
    )(tokens, gain[None])


def join_cores(place, own, partner, stream, piece, after):
    rows = own.shape[0]

    def kernel(place_ref, own_ref, partner_ref, *rest):
        core = place_ref[place_ref.shape[0] - 1]
        out_ref = rest[-1]
        out_ref[pl.ds(pl.multiple_of(core * rows, rows), rows), :] = own_ref[...]
        out_ref[pl.ds(pl.multiple_of((1 - core) * rows, rows), rows), :] = partner_ref[...]

    part = pl.BlockSpec((rows, piece), lambda i, place_ref: (0, stream))
    return call(
        kernel,
        place,
        (1,),
        [part, part] + [pl.BlockSpec(memory_space=pl.ANY)] * len(after),
        pl.BlockSpec((2 * rows, piece), lambda i, place_ref: (0, 0)),
        jax.ShapeDtypeStruct((2 * rows, piece), jnp.bfloat16),
        0,
        8 * rows * piece,
    )(place, own, partner, *after)


def project(place, x, pieces, other, chips):
    rows, model = x.shape
    block = model // chips
    piece = pieces[0].shape[1]

    def kernel(place_ref, x_ref, *refs):
        piece_refs, other_ref, out_ref, weight, total = refs[:chips], *refs[chips:]
        step = pl.program_id(0)
        position = place_ref[chips]

        @pl.when(step == 0)
        def _():
            total[...] = jnp.zeros_like(total)
            weight[0] = piece_refs[0][...]
            for p in range(1, chips):

                @pl.when(position >= p)
                def _():
                    weight[p] = piece_refs[p][...]

                @pl.when(position < p)
                def _():
                    weight[p] = other_ref[chips - p - 1]

        total[...] += jnp.dot(x_ref[...], weight[step], preferred_element_type=jnp.float32)

        @pl.when(step == chips - 1)
        def _():
            out_ref[...] = total[...].astype(jnp.bfloat16).T

    whole = pl.BlockSpec((block, piece), lambda i, place_ref: (0, 0))
    return call(
        kernel,
        place,
        (chips,),
        [pl.BlockSpec((rows, block), lambda i, place_ref: (0, place_ref[i]))]
        + [whole] * chips
        + [pl.BlockSpec((chips - 1, block, piece), lambda i, place_ref: (0, 0, 0))],
        pl.BlockSpec((piece, rows), lambda i, place_ref: (0, 0)),
        jax.ShapeDtypeStruct((piece, rows), jnp.bfloat16),
        2 * rows * model * piece,
        2 * rows * model + 4 * model * piece,
        [pltpu.VMEM((chips, block, piece), jnp.bfloat16), pltpu.VMEM((rows, piece), jnp.float32)],
    )(place, x, *pieces, other)


def gradient(place, mid, x, chips, first, count):
    piece, rows = mid.shape
    block = x.shape[1] // chips

    def kernel(place_ref, mid_ref, x_ref, out_ref):
        term = jnp.dot(mid_ref[...], x_ref[...], preferred_element_type=jnp.float32)
        out_ref[0] = term.astype(jnp.bfloat16).T

    return call(
        kernel,
        place,
        (count,),
        [
            pl.BlockSpec((piece, rows), lambda i, place_ref: (0, 0)),
            pl.BlockSpec((rows, block), lambda i, place_ref: (0, place_ref[first + i])),
        ],
        pl.BlockSpec((1, block, piece), lambda i, place_ref: (i, 0, 0)),
        jax.ShapeDtypeStruct((count, block, piece), jnp.bfloat16),
        2 * rows * block * count * piece,
        2 * rows * block * count + 2 * count * block * piece,
    )(place, mid, x)


def per_device(
    tokens,
    norm_gain,
    value_weight,
    output_weight,
    out_cotangent,
    base_params,
    outer_momentum,
    delta_values,
    delta_exponents,
):
    replicas = lax.axis_size("replica")
    devices = lax.axis_size("fsdp")
    chips = devices // 2
    me = lax.axis_index("fsdp")
    chip, core = me // 2, me % 2
    position = jnp.where(core == 0, chip, chips - 1 - chip)
    back = jnp.arange(chips, dtype=jnp.int32)
    behind = jnp.where(core == 0, chip - back + chips, chip + back) % chips
    place = jnp.concatenate([behind, position[None], core[None]]).astype(jnp.int32)

    def swap(value):
        return lax.ppermute(value, "fsdp", [(i, i ^ 1) for i in range(devices)])

    def move(value, active=lambda y: True):
        return lax.ppermute(value, "fsdp", move_perm(chips, active))

    shard = value_weight.shape[1]
    piece = value_weight.shape[2] // STREAMS
    streams = range(STREAMS)
    first_own, second_own = value_weight[0], output_weight[0]
    first_partner, second_partner = swap(first_own), swap(second_own)

    scaled = (
        delta_values[0].astype(jnp.float32)
        * jnp.exp2(delta_exponents[0].astype(jnp.float32))[:, None]
    )
    delta = lax.psum(scaled.astype(jnp.bfloat16), "replica").astype(jnp.float32) * (1.0 / replicas)

    normed = normalise(tokens[0], norm_gain)
    cotangent = out_cotangent[0]

    def partial(rest, other, step, received):
        term = rest[step - 1].astype(jnp.float32) + other[chips - step - 1].astype(jnp.float32)
        if received is not None:
            term = term + received.astype(jnp.float32)
        return term.astype(jnp.bfloat16)

    def terms(x_in, x_out, pieces):
        other = swap(jnp.stack(pieces[1:]))
        mid = project(place, x_in, pieces, other, chips)
        rest = gradient(place, mid, x_out, chips, 1, chips - 1)
        return (rest, swap(rest), gradient(place, mid, x_out, chips, 0, 1)[0])

    def finish(here, received):
        whole = here.astype(jnp.float32) + received.astype(jnp.float32)
        mine = lax.dynamic_slice_in_dim(whole, core * shard, shard, 0)
        partners = lax.dynamic_slice_in_dim(whole, (1 - core) * shard, shard, 0)
        return mine + swap(partners.astype(jnp.bfloat16)).astype(jnp.float32)

    held = [[join_cores(place, first_own, first_partner, j, piece, ())] for j in streams]
    for step in range(1, chips):
        for j in streams:
            held[j].append(move(held[j][-1], lambda y: y >= step - 1))
    sent = [
        join_cores(place, second_own, second_partner, j, piece, (held[j][-1],)) for j in streams
    ]
    first = [terms(normed, cotangent, held[j]) for j in streams]
    later = [[sent[j]] for j in streams]
    received = [move(sent[j]) for j in streams]
    for step in range(1, chips):
        for j in streams:
            later[j].append(received[j])
            rest, other, _ = first[j]
            message = jnp.where(
                position >= step, received[j], partial(rest, other, step, received[j])
            )
            received[j] = move(message)
    output_grad = [finish(first[j][2], received[j]) for j in streams]
    second = [terms(cotangent, normed, later[j]) for j in streams]
    received = [None] * STREAMS
    for step in range(1, chips):
        for j in streams:
            rest, other, _ = second[j]
            message = partial(rest, other, step, received[j])
            received[j] = move(message, lambda y: y <= step - 1)
    value_grad = [finish(second[j][2], received[j]) for j in streams]

    new_base, new_momentum = nesterov(delta, base_params, outer_momentum)
    return (
        jnp.concatenate(value_grad, axis=1)[None],
        jnp.concatenate(output_grad, axis=1)[None],
        new_base,
        new_momentum,
    )


def solution(mesh):
    return jax.shard_map(
        per_device,
        mesh=mesh,
        in_specs=(
            P("replica", "fsdp", None),
            P(),
            P("replica", "fsdp", None),
            P("replica", "fsdp", None),
            P("replica", "fsdp", None),
            P("fsdp", None),
            P("fsdp", None),
            P("replica", "fsdp", None),
            P("replica", "fsdp"),
        ),
        out_specs=(
            P("replica", "fsdp", None),
            P("replica", "fsdp", None),
            P("fsdp", None),
            P("fsdp", None),
        ),
        check_vma=False,
    )
```

```python
import jax
import jax.numpy as jnp
from jax import lax
from jax.experimental import pallas as pl
from jax.experimental.pallas import tpu as pltpu
from jax.sharding import PartitionSpec as P

STREAMS = 2
ROW_TILE = 128
FLOPS_PER_US = 20 * 10**9
VMEM_LIMIT = 57 * 1024 * 1024


def move_perm(chips, active):
    pairs = []
    for z in range(chips):
        if z < chips - 1 and active(z):
            pairs.append((2 * z, 2 * z + 2))
        if z > 0 and active(chips - 1 - z):
            pairs.append((2 * z + 1, 2 * z - 1))
    return pairs


class Order:
    def __init__(self, place):
        self.place = place
        self.last = ()

    def __call__(
        self, kernel, args, grid, in_specs, out_specs, out_shape, after=(), scratch=(), aliases=None, us=0.0
    ):
        after = tuple(x for x in self.last + tuple(after) if all(x is not y for y in args))
        count = len(args)
        name = kernel.__qualname__.split(".")[0]

        def ordered(place_ref, *refs):
            kernel(place_ref, *refs[:count], *refs[count + len(after) :])

        result = pl.pallas_call(
            ordered,
            grid_spec=pltpu.PrefetchScalarGridSpec(
                num_scalar_prefetch=1,
                grid=grid,
                in_specs=in_specs + [pl.BlockSpec(memory_space=pl.ANY)] * len(after),
                out_specs=out_specs,
                scratch_shapes=scratch,
            ),
            out_shape=out_shape,
            input_output_aliases={1 + i: o for i, o in (aliases or {}).items()},
            compiler_params=pltpu.CompilerParams(vmem_limit_bytes=VMEM_LIMIT),
            cost_estimate=pl.CostEstimate(flops=int(us * FLOPS_PER_US) + 1, bytes_accessed=1, transcendentals=0),
            name=name,
        )(self.place, *args, *after)
        self.last = (result[0] if isinstance(result, (list, tuple)) else result,)
        return result


def normalise(order, tokens, gain, after):
    rows, model = tokens.shape

    def run(_, tokens_ref, gain_ref, out_ref):
        xf = tokens_ref[...].astype(jnp.float32)
        scale = lax.rsqrt(jnp.mean(xf * xf, axis=1, keepdims=True) + 1e-05)
        out_ref[...] = (xf * scale * gain_ref[...]).astype(jnp.bfloat16)

    tile = pl.BlockSpec((ROW_TILE, model), lambda i, _: (i, 0))
    return order(
        run,
        (tokens, gain[None]),
        (rows // ROW_TILE,),
        [tile, pl.BlockSpec((1, model), lambda i, _: (0, 0))],
        tile,
        jax.ShapeDtypeStruct((rows, model), jnp.bfloat16),
        after,
        us=5.0,
    )


def join_cores(order, own, partner, after):
    rows, features = own.shape
    piece = features // STREAMS

    def join_cores(place_ref, own_ref, partner_ref, *out_refs):
        core = place_ref[place_ref.shape[0] - 1]
        for j, out_ref in enumerate(out_refs):
            cols = slice(j * piece, (j + 1) * piece)
            out_ref[pl.ds(pl.multiple_of(core * rows, rows), rows), :] = own_ref[:, cols]
            out_ref[pl.ds(pl.multiple_of((1 - core) * rows, rows), rows), :] = partner_ref[:, cols]

    part = pl.BlockSpec((rows, features), lambda i, _: (0, 0))
    return order(
        join_cores,
        (own, partner),
        (1,),
        [part, part],
        [pl.BlockSpec((2 * rows, piece), lambda i, _: (0, 0))] * STREAMS,
        [jax.ShapeDtypeStruct((2 * rows, piece), jnp.bfloat16)] * STREAMS,
        after,
        us=0.6,
    )


def project(order, x, pieces, others, after=()):
    chips, parts = len(pieces), len(pieces[0])
    rows, model = x.shape
    block = model // chips
    piece = pieces[0][0].shape[1]
    wide = parts * piece

    def run(place_ref, x_ref, *refs):
        piece_refs = [refs[p * parts : (p + 1) * parts] for p in range(chips)]
        refs = refs[chips * parts :]
        other_refs = [refs[p * parts : (p + 1) * parts] for p in range(chips - 1)]
        out_ref, weight, total = refs[(chips - 1) * parts :]
        step = pl.program_id(0)
        position = place_ref[chips]

        def fill(p, source):
            for j in range(parts):
                weight[p, :, j * piece : (j + 1) * piece] = source[j][...]

        @pl.when(step == 0)
        def _():
            total[...] = jnp.zeros_like(total)
            fill(0, piece_refs[0])
            for p in range(1, chips):
                pl.when(position >= p)(lambda p=p: fill(p, piece_refs[p]))
                pl.when(position < p)(lambda p=p: fill(p, other_refs[chips - p - 1]))

        total[...] += jnp.dot(x_ref[...], weight[step], preferred_element_type=jnp.float32)

        @pl.when(step == chips - 1)
        def _():
            out_ref[...] = total[...].astype(jnp.bfloat16).T

    whole = pl.BlockSpec((block, piece), lambda i, _: (0, 0))
    arrays = [part for shard in (*pieces, *others) for part in shard]
    return order(
        run,
        (x, *arrays),
        (chips,),
        [pl.BlockSpec((rows, block), lambda i, place_ref: (0, place_ref[i]))]
        + [whole] * len(arrays),
        pl.BlockSpec((wide, rows), lambda i, _: (0, 0)),
        jax.ShapeDtypeStruct((wide, rows), jnp.bfloat16),
        after,
        [pltpu.VMEM((chips, block, wide), jnp.bfloat16), pltpu.VMEM((rows, wide), jnp.float32)],
        us=4.4,
    )


def gradient(order, mid, x, chips, first, count, after=()):
    piece, rows = mid.shape
    block = x.shape[1] // chips

    def run(_, mid_ref, x_ref, out_ref):
        term = jnp.dot(mid_ref[...], x_ref[...], preferred_element_type=jnp.float32)
        out_ref[0] = term.astype(jnp.bfloat16).T

    return order(
        run,
        (mid, x),
        (count,),
        [
            pl.BlockSpec((piece, rows), lambda i, _: (0, 0)),
            pl.BlockSpec((rows, block), lambda i, place_ref: (0, place_ref[first + i])),
        ],
        pl.BlockSpec((1, block, piece), lambda i, _: (i, 0, 0)),
        jax.ShapeDtypeStruct((count, block, piece), jnp.bfloat16),
        after,
        us=1.2 * count,
    )


def nesterov(order, share, shares, replicas, sums, base, momentum, held, after):
    rows, lanes = base.shape
    tile = rows // shares // 2
    count = len(sums)

    def run(_, *refs):
        base_ref, momentum_ref = refs[count : count + 2]
        base_out, momentum_out = refs[-2:]
        total = refs[0][...].astype(jnp.float32)
        for ref in refs[1:count]:
            total = total + ref[...].astype(jnp.float32)
        delta = total * (1.0 / replicas)
        momentum_next = 0.9 * momentum_ref[...] + delta
        momentum_out[...] = momentum_next
        base_out[...] = (
            base_ref[...].astype(jnp.float32) - 0.7 * (delta + 0.9 * momentum_next)
        ).astype(jnp.bfloat16)

    spec = pl.BlockSpec((tile, lanes), lambda i, _: (2 * share + i, 0))
    first = 2 * (share % (shares // 2))
    own = pl.BlockSpec((tile, lanes), lambda i, _: (first + i, 0))
    return order(
        run,
        (*sums, base, momentum, *held),
        (2,),
        [own] * count + [spec] * 2 + [pl.BlockSpec(memory_space=pl.ANY)] * len(held),
        [spec] * 2,
        [
            jax.ShapeDtypeStruct((rows, lanes), jnp.bfloat16),
            jax.ShapeDtypeStruct((rows, lanes), jnp.float32),
        ],
        after,
        aliases={count + 2: 0, count + 3: 1} if held else None,
        us=1.7,
    )


def per_device(
    tokens,
    norm_gain,
    value_weight,
    output_weight,
    out_cotangent,
    base_params,
    outer_momentum,
    delta_values,
    delta_exponents,
):
    replicas = lax.axis_size("replica")
    devices = lax.axis_size("fsdp")
    chips = devices // 2
    me = lax.axis_index("fsdp")
    chip, core = me // 2, me % 2
    position = jnp.where(core == 0, chip, chips - 1 - chip)
    back = jnp.arange(chips, dtype=jnp.int32)
    behind = jnp.where(core == 0, chip - back + chips, chip + back) % chips
    order = Order(jnp.concatenate([behind, position[None], core[None]]).astype(jnp.int32))
    shard = value_weight.shape[1]
    cotangent = out_cotangent[0]

    def swap(value):
        return lax.ppermute(value, "fsdp", [(i, i ^ 1) for i in range(devices)])

    def move(value, active=lambda y: True):
        return lax.ppermute(value, "fsdp", move_perm(chips, active))

    class Part:
        def __init__(self, own):
            self.own = own
            self.pieces, self.others = [[part] for part in own], []

        def gather(self, step):
            for pieces in self.pieces:
                pieces.append(move(pieces[-1], lambda y: y >= step - 1))
            self.others.append([swap(pieces[-1]) for pieces in self.pieces])

        def project(self, x, after=()):
            pieces = [list(shard) for shard in zip(*self.pieces)]
            self.mid = project(order, x, pieces, self.others, after)

        def terms(self, x, after=()):
            self.rest = gradient(order, self.mid, x, chips, 1, chips - 1, after)
            self.across = swap(self.rest)

        def term_here(self, x, after=()):
            self.here = gradient(order, self.mid, x, chips, 0, 1, after)[0]

        def reduce(self, step):
            term = self.rest[step - 1].astype(jnp.float32)
            term = term + self.across[chips - step - 1].astype(jnp.float32)
            if step > 1:
                term = term + self.arrived.astype(jnp.float32)
            message = term.astype(jnp.bfloat16)
            self.arrived = move(message, lambda y: y <= step - 1)
            return message

        def finish(self):
            whole = self.here.astype(jnp.float32) + self.arrived.astype(jnp.float32)
            mine = lax.dynamic_slice_in_dim(whole, core * shard, shard, 0)
            partners = lax.dynamic_slice_in_dim(whole, (1 - core) * shard, shard, 0)
            return mine + swap(partners.astype(jnp.bfloat16)).astype(jnp.float32)

    first_own, second_own = value_weight[0], output_weight[0]
    first_partner, second_partner = swap(first_own), swap(second_own)

    bits = replicas.bit_length() - 1
    if replicas != 1 << bits or bits < 1:
        raise ValueError("replicas")
    half = base_params.shape[0] // 2
    sums, early = [], []
    for index in range(2):
        rows = slice(index * half, (index + 1) * half)
        scale = jnp.exp2(delta_exponents[0, rows].astype(jnp.float32))[:, None]
        total = delta_values[0, rows].astype(jnp.float32) * scale
        for turn in range(bits):
            mine = total.astype(jnp.bfloat16)
            bit = 1 << ((turn + index) % bits)
            theirs = lax.ppermute(mine, "replica", [(i, i ^ bit) for i in range(replicas)])
            total = mine.astype(jnp.float32) + theirs.astype(jnp.float32)
            if turn == 0:
                early.append(theirs)
        sums.append((mine, theirs))
    outer = ()
    shares = 4

    def outer_step(share, after=()):
        nonlocal outer
        outer = nesterov(
            order, share, shares, replicas, sums[share * 2 // shares], base_params,
            outer_momentum, outer, after,
        )

    joined = join_cores(order, first_own, first_partner, (second_partner,))
    v = Part(joined)
    for step in range(1, chips):
        v.gather(step)
    normed = normalise(order, tokens[0], norm_gain, ())

    joined = join_cores(order, second_own, second_partner, (v.pieces[0][-1],))
    oa, ob = Part(joined[:1]), Part(joined[1:])
    for step in range(1, chips):
        oa.gather(step)
        ob.gather(step)
    v.project(normed, early)
    v.terms(cotangent, (oa.pieces[0][1],))
    sent = [v.reduce(step) for step in range(1, chips)]
    v.term_here(cotangent, sent[:1])
    output_grad = v.finish()
    oa.project(cotangent, sent[1:2])
    oa.terms(normed)
    ob.project(cotangent, sent[2:3])
    ob.terms(normed)
    oa.term_here(normed)
    ob.term_here(normed)

    share = 0
    for step in range(1, chips):
        for part in (oa, ob):
            sent = part.reduce(step)
            if step > 1 and share < shares:
                outer_step(share, (sent,))
                share += 1
    value_grad = jnp.concatenate([oa.finish(), ob.finish()], axis=1)
    return (value_grad[None], output_grad[None], *outer)


def solution(mesh):
    return jax.shard_map(
        per_device,
        mesh=mesh,
        in_specs=(
            P("replica", "fsdp", None),
            P(),
            P("replica", "fsdp", None),
            P("replica", "fsdp", None),
            P("replica", "fsdp", None),
            P("fsdp", None),
            P("fsdp", None),
            P("replica", "fsdp", None),
            P("replica", "fsdp"),
        ),
        out_specs=(
            P("replica", "fsdp", None),
            P("replica", "fsdp", None),
            P("fsdp", None),
            P("fsdp", None),
        ),
        check_vma=False,
    )
```

```python
import jax
import jax.numpy as jnp
from jax import lax
from jax.experimental import pallas as pl
from jax.experimental.pallas import tpu as pltpu
from jax.sharding import PartitionSpec as P

STREAMS = 2
KERNEL_FLOPS = 20 * 10**9
HBM = pl.BlockSpec(memory_space=pltpu.HBM)
ANY = pl.BlockSpec(memory_space=pl.ANY)


def move_perm(chips, active):
    pairs = []
    for z in range(chips):
        if z < chips - 1 and active(z):
            pairs.append((2 * z, 2 * z + 2))
        if z > 0 and active(chips - 1 - z):
            pairs.append((2 * z + 1, 2 * z - 1))
    return pairs


class Order:
    def __init__(self, place):
        self.place = place
        self.last = ()

    def __call__(self, kernel, args, in_specs, out_shape, scratch, vmem, after=(), aliases=None):
        after = self.last + tuple(after)
        count = len(args)

        def ordered(place_ref, *refs):
            kernel(place_ref, *refs[:count], *refs[count + len(after) :])

        result = pl.pallas_call(
            ordered,
            grid_spec=pltpu.PrefetchScalarGridSpec(
                num_scalar_prefetch=1,
                grid=(1,),
                in_specs=in_specs + [ANY] * len(after),
                out_specs=[HBM] * len(out_shape),
                scratch_shapes=scratch,
            ),
            out_shape=out_shape,
            input_output_aliases={1 + i: o for i, o in (aliases or {}).items()},
            compiler_params=pltpu.CompilerParams(vmem_limit_bytes=vmem * 1024 * 1024),
            cost_estimate=pl.CostEstimate(flops=KERNEL_FLOPS, bytes_accessed=1, transcendentals=0),
            name=kernel.__qualname__.split(".")[0],
        )(self.place, *args, *after)
        self.last = (result[0],)
        return result


def copies(pairs, sems):
    started = [pltpu.make_async_copy(a, b, sems.at[i]) for i, (a, b) in enumerate(pairs)]
    for copy in started:
        copy.start()
    return started


def normalise(order, tokens, gain, after=()):
    rows, model = tokens.shape
    tiles = 8
    tile = rows // tiles

    def run(_, tokens_ref, gain_ref, out_ref, held, done, in_sems, out_sems):
        def place(ref, i):
            return ref.at[pl.ds(pl.multiple_of(i * tile, tile), tile)]

        def arrive(i):
            return pltpu.make_async_copy(place(tokens_ref, i), place(held, i), in_sems.at[i])

        def leave(i):
            return pltpu.make_async_copy(place(done, i), place(out_ref, i), out_sems.at[i])

        for i in range(tiles):
            arrive(i).start()

        def step(i, carry):
            arrive(i).wait()
            xf = place(held, i)[...].astype(jnp.float32)
            scale = lax.rsqrt(jnp.mean(xf * xf, axis=1, keepdims=True) + 1e-05)
            place(done, i)[...] = (xf * scale * gain_ref[...]).astype(jnp.bfloat16)
            leave(i).start()
            return carry

        lax.fori_loop(0, tiles, step, 0)
        for i in range(tiles):
            leave(i).wait()

    return order(
        run,
        (tokens, gain[None]),
        [HBM, pl.BlockSpec((1, model), lambda i, _: (0, 0))],
        [jax.ShapeDtypeStruct((rows, model), jnp.bfloat16)],
        [
            pltpu.VMEM((rows, model), jnp.bfloat16),
            pltpu.VMEM((rows, model), jnp.bfloat16),
            pltpu.SemaphoreType.DMA((tiles,)),
            pltpu.SemaphoreType.DMA((tiles,)),
        ],
        28,
        after,
    )[0]


def join_cores(order, own, partner, after=()):
    rows, features = own.shape
    piece = features // STREAMS

    def run(place_ref, own_ref, partner_ref, *refs):
        out_refs, sems = refs[:STREAMS], refs[STREAMS]
        core = place_ref[place_ref.shape[0] - 1]
        pairs = []
        for j, out_ref in enumerate(out_refs):
            cols = pl.ds(j * piece, piece)
            for source, where in ((own_ref, core), (partner_ref, 1 - core)):
                target = out_ref.at[pl.ds(pl.multiple_of(where * rows, rows), rows)]
                pairs.append((source.at[:, cols], target))
        for copy in copies(pairs, sems):
            copy.wait()

    return order(
        run,
        (own, partner),
        [HBM, ANY],
        [jax.ShapeDtypeStruct((2 * rows, piece), jnp.bfloat16)] * STREAMS,
        [pltpu.SemaphoreType.DMA((2 * STREAMS,))],
        4,
        after,
    )


def products(order, x_in, x_out, pieces, others, after=()):
    chips = len(pieces)
    rows, model = x_in.shape
    block = model // chips
    piece = pieces[0].shape[1]
    places = [*range(1, chips), 0]

    def run(place_ref, in_ref, out_ref, *refs):
        piece_refs, other_refs = refs[:chips], refs[chips : 2 * chips - 1]
        rest_ref, here_ref, held_in, held_out, weight, total, mid, term, *sems = refs[2 * chips - 1 :]
        position = place_ref[chips]

        def columns(p):
            return pl.ds(pl.multiple_of(place_ref[p] * block, block), block)

        def shard(source, p):
            return pltpu.make_async_copy(source, weight.at[p], sems[0].at[p])

        def arrive_in(p):
            return pltpu.make_async_copy(in_ref.at[:, columns(p)], held_in.at[p], sems[1].at[p])

        def arrive_out(p):
            return pltpu.make_async_copy(out_ref.at[:, columns(p)], held_out.at[p], sems[2].at[p])

        def leave(p):
            target = rest_ref.at[p - 1] if p else here_ref
            return pltpu.make_async_copy(term.at[p], target, sems[3].at[p])

        shard(piece_refs[0], 0).start()
        arrive_in(0).start()
        for p in range(1, chips):
            pl.when(position >= p)(lambda p=p: shard(piece_refs[p], p).start())
            pl.when(position < p)(lambda p=p: shard(other_refs[chips - p - 1], p).start())
            arrive_in(p).start()
        for p in places:
            arrive_out(p).start()
        for p in range(chips):
            shard(piece_refs[0], p).wait()
            arrive_in(p).wait()
            part = jnp.dot(held_in[p], weight[p], preferred_element_type=jnp.float32)
            total[...] = part if p == 0 else total[...] + part
        mid[...] = total[...].astype(jnp.bfloat16).T
        for p in places:
            arrive_out(p).wait()
            part = jnp.dot(mid[...], held_out[p], preferred_element_type=jnp.float32)
            term[p] = part.astype(jnp.bfloat16).T
            leave(p).start()
        for p in places:
            leave(p).wait()

    bf16 = jnp.bfloat16
    return order(
        run,
        (x_in, x_out, *pieces, *others),
        [HBM, HBM] + [ANY] * (2 * chips - 1),
        [
            jax.ShapeDtypeStruct((chips - 1, block, piece), bf16),
            jax.ShapeDtypeStruct((block, piece), bf16),
        ],
        [
            pltpu.VMEM((chips, rows, block), bf16),
            pltpu.VMEM((chips, rows, block), bf16),
            pltpu.VMEM((chips, block, piece), bf16),
            pltpu.VMEM((rows, piece), jnp.float32),
            pltpu.VMEM((piece, rows), bf16),
            pltpu.VMEM((chips, block, piece), bf16),
        ]
        + [pltpu.SemaphoreType.DMA((chips,))] * 4,
        32,
        after,
    )


def outer_step(order, replicas, sums, base, momentum, passing, after=()):
    rows, lanes = base.shape
    tiles = 8
    tile = rows // tiles
    ranges = len(sums)
    parts = [part for pair in sums for part in pair]

    def run(_, *refs):
        part_refs = refs[: 2 * ranges]
        base_ref, momentum_ref, _, base_out, momentum_out, _ = refs[2 * ranges : 2 * ranges + 6]
        mine, theirs, base_held, held, base_next, next_, *sems = refs[2 * ranges + 6 :]

        def arrive(i):
            pair = 2 * (i * ranges // tiles)
            first = (i - i * ranges // tiles * tiles // ranges) * tile
            own, to = pl.ds(first, tile), pl.ds(i * tile, tile)
            moves = (
                (part_refs[pair].at[own], mine.at[to]),
                (part_refs[pair + 1].at[own], theirs.at[to]),
                (base_ref.at[to], base_held.at[to]),
                (momentum_ref.at[to], held.at[to]),
            )
            return [pltpu.make_async_copy(a, b, s.at[i]) for (a, b), s in zip(moves, sems)]

        def leave(i):
            at = pl.ds(i * tile, tile)
            moves = ((base_next.at[at], base_out.at[at]), (next_.at[at], momentum_out.at[at]))
            return [pltpu.make_async_copy(a, b, s.at[i]) for (a, b), s in zip(moves, sems[4:])]

        for i in range(tiles):
            for copy in arrive(i):
                copy.start()
        for i in range(tiles):
            for copy in arrive(i):
                copy.wait()
            at = slice(i * tile, (i + 1) * tile)
            total = mine[at].astype(jnp.float32) + theirs[at].astype(jnp.float32)
            delta = total * (1.0 / replicas)
            momentum_next = 0.9 * held[at] + delta
            next_[at] = momentum_next
            base_next[at] = (
                base_held[at].astype(jnp.float32) - 0.7 * (delta + 0.9 * momentum_next)
            ).astype(jnp.bfloat16)
            for copy in leave(i):
                copy.start()
        for i in range(tiles):
            for copy in leave(i):
                copy.wait()

    half, full = pltpu.VMEM((rows, lanes), jnp.bfloat16), pltpu.VMEM((rows, lanes), jnp.float32)
    return order(
        run,
        (*parts, base, momentum, passing),
        [ANY] * (2 * ranges) + [HBM] * 3,
        [
            jax.ShapeDtypeStruct((rows, lanes), jnp.bfloat16),
            jax.ShapeDtypeStruct((rows, lanes), jnp.float32),
            jax.ShapeDtypeStruct(passing.shape, passing.dtype),
        ],
        [half, half, half, full, half, full] + [pltpu.SemaphoreType.DMA((tiles,))] * 6,
        24,
        after,
        {2 * ranges + 2: 2},
    )


def per_device(
    tokens,
    norm_gain,
    value_weight,
    output_weight,
    out_cotangent,
    base_params,
    outer_momentum,
    delta_values,
    delta_exponents,
):
    replicas = lax.axis_size("replica")
    devices = lax.axis_size("fsdp")
    chips = devices // 2
    me = lax.axis_index("fsdp")
    chip, core = me // 2, me % 2
    position = jnp.where(core == 0, chip, chips - 1 - chip)
    back = jnp.arange(chips, dtype=jnp.int32)
    behind = jnp.where(core == 0, chip - back + chips, chip + back) % chips
    order = Order(jnp.concatenate([behind, position[None], core[None]]).astype(jnp.int32))
    shard = value_weight.shape[1]
    cotangent = out_cotangent[0]

    def swap(value):
        return lax.ppermute(value, "fsdp", [(i, i ^ 1) for i in range(devices)])

    def move(value, active=lambda y: True):
        return lax.ppermute(value, "fsdp", move_perm(chips, active))

    class Part:
        def __init__(self, own):
            self.pieces, self.others = [own], []

        def gather(self, step):
            self.pieces.append(move(self.pieces[-1], lambda y: y >= step - 1))
            self.others.append(swap(self.pieces[-1]))

        def products(self, x_in, x_out, after=()):
            self.rest, self.here = products(order, x_in, x_out, self.pieces, self.others, after)
            self.across = swap(self.rest)

        def reduce(self, step):
            term = self.rest[step - 1].astype(jnp.float32)
            term = term + self.across[chips - step - 1].astype(jnp.float32)
            if step > 1:
                term = term + self.arrived.astype(jnp.float32)
            message = term.astype(jnp.bfloat16)
            self.arrived = move(message, lambda y: y <= step - 1)
            return message

        def finish(self):
            whole = self.here.astype(jnp.float32) + self.arrived.astype(jnp.float32)
            mine = lax.dynamic_slice_in_dim(whole, core * shard, shard, 0)
            partners = lax.dynamic_slice_in_dim(whole, (1 - core) * shard, shard, 0)
            return mine + swap(partners.astype(jnp.bfloat16)).astype(jnp.float32)

    first_own, second_own = value_weight[0], output_weight[0]
    first_partner, second_partner = swap(first_own), swap(second_own)

    bits = replicas.bit_length() - 1
    if replicas != 1 << bits or bits < 1:
        raise ValueError("replicas")
    half = base_params.shape[0] // 2
    sums, early = [], []
    for index in range(2):
        rows = slice(index * half, (index + 1) * half)
        scale = jnp.exp2(delta_exponents[0, rows].astype(jnp.float32))[:, None]
        total = delta_values[0, rows].astype(jnp.float32) * scale
        for turn in range(bits):
            mine = total.astype(jnp.bfloat16)
            bit = 1 << ((turn + index) % bits)
            theirs = lax.ppermute(mine, "replica", [(i, i ^ bit) for i in range(replicas)])
            total = mine.astype(jnp.float32) + theirs.astype(jnp.float32)
            if turn == 0:
                early.append(theirs)
        sums.append((mine, theirs))

    va, vb = (Part(own) for own in join_cores(order, first_own, first_partner, (second_partner,)))
    for step in range(1, chips):
        va.gather(step)
        vb.gather(step)
    normed = normalise(order, tokens[0], norm_gain)

    joined = join_cores(order, second_own, second_partner, (va.pieces[-1],))
    oa, ob = (Part(own) for own in joined)
    for step in range(1, chips):
        oa.gather(step)
        ob.gather(step)
    va.products(normed, cotangent)
    vb.products(normed, cotangent, (oa.pieces[1], ob.pieces[1], *early))
    sent = [(va.reduce(step), vb.reduce(step)) for step in range(1, chips)]
    output_grad = jnp.concatenate([va.finish(), vb.finish()], axis=1)
    oa.products(cotangent, normed, sent[1])
    ob.products(cotangent, normed, (*sent[2], sums[0][1], sums[1][1]))

    sent = [(oa.reduce(step), ob.reduce(step)) for step in range(1, chips)]
    new_base, new_momentum, oa.here = outer_step(
        order, replicas, sums, base_params, outer_momentum, oa.here, sent[1]
    )
    value_grad = jnp.concatenate([oa.finish(), ob.finish()], axis=1)
    return (value_grad[None], output_grad[None], new_base, new_momentum)


def solution(mesh):
    return jax.shard_map(
        per_device,
        mesh=mesh,
        in_specs=(
            P("replica", "fsdp", None),
            P(),
            P("replica", "fsdp", None),
            P("replica", "fsdp", None),
            P("replica", "fsdp", None),
            P("fsdp", None),
            P("fsdp", None),
            P("replica", "fsdp", None),
            P("replica", "fsdp"),
        ),
        out_specs=(
            P("replica", "fsdp", None),
            P("replica", "fsdp", None),
            P("fsdp", None),
            P("fsdp", None),
        ),
        check_vma=False,
    )
```

```python
import jax
import jax.numpy as jnp
from jax import lax
from jax.experimental import pallas as pl
from jax.experimental.pallas import tpu as pltpu
from jax.sharding import PartitionSpec as P

HALVES = 2
ROW_TILE = 128
KERNEL_FLOPS = 20 * 10**9
ANY = pl.BlockSpec(memory_space=pl.ANY)


def move_perm(chips, active):
    pairs = []
    for z in range(chips):
        if z < chips - 1 and active(z):
            pairs.append((2 * z, 2 * z + 2))
        if z > 0 and active(chips - 1 - z):
            pairs.append((2 * z + 1, 2 * z - 1))
    return pairs


class Order:
    def __init__(self, place):
        self.place = place
        self.last = ()

    def __call__(
        self, kernel, args, in_specs, out_shape, scratch, vmem, after=(), aliases=None, grid=1,
        out_specs=None,
    ):
        after = self.last + tuple(after)
        count = len(args)

        def ordered(place_ref, *refs):
            kernel(place_ref, *refs[:count], *refs[count + len(after) :])

        result = pl.pallas_call(
            ordered,
            grid_spec=pltpu.PrefetchScalarGridSpec(
                num_scalar_prefetch=1,
                grid=(grid,),
                in_specs=in_specs + [ANY] * len(after),
                out_specs=out_specs or [ANY] * len(out_shape),
                scratch_shapes=scratch,
            ),
            out_shape=out_shape,
            input_output_aliases={1 + i: o for i, o in (aliases or {}).items()},
            compiler_params=pltpu.CompilerParams(vmem_limit_bytes=vmem * 1024 * 1024),
            cost_estimate=pl.CostEstimate(flops=KERNEL_FLOPS, bytes_accessed=1, transcendentals=0),
            name=kernel.__qualname__.split(".")[0],
        )(self.place, *args, *after)
        self.last = (result[0],)
        return result


def copies(pairs, sems):
    started = [pltpu.make_async_copy(a, b, sems.at[i]) for i, (a, b) in enumerate(pairs)]
    for copy in started:
        copy.start()
    return started


def fence(order, *values, after=()):
    def fence(*refs):
        pass

    shapes = [jax.ShapeDtypeStruct(v.shape, v.dtype) for v in values]
    aliases = {i: i for i in range(len(values))}
    return order(fence, values, [ANY] * len(values), shapes, [], 4, after, aliases)


def normalise(order, tokens, gain, after=()):
    rows, model = tokens.shape

    def run(_, tokens_ref, gain_ref, out_ref):
        xf = tokens_ref[...].astype(jnp.float32)
        scale = lax.rsqrt(jnp.mean(xf * xf, axis=1, keepdims=True) + 1e-05)
        out_ref[...] = (xf * scale * gain_ref[...]).astype(jnp.bfloat16)

    tile = pl.BlockSpec((ROW_TILE, model), lambda i, _: (i, 0))
    return order(
        run,
        (tokens, gain[None]),
        [tile, pl.BlockSpec((1, model), lambda i, _: (0, 0))],
        [jax.ShapeDtypeStruct((rows, model), jnp.bfloat16)],
        [],
        16,
        after,
        grid=rows // ROW_TILE,
        out_specs=[tile],
    )[0]


def join_cores(order, own, partner, after=()):
    rows, features = own.shape
    piece = features // HALVES

    def run(place_ref, own_ref, partner_ref, *refs):
        out_refs, sems = refs[:HALVES], refs[HALVES]
        core = place_ref[place_ref.shape[0] - 1]
        pairs = []
        for j, out_ref in enumerate(out_refs):
            cols = pl.ds(j * piece, piece)
            for source, where in ((own_ref, core), (partner_ref, 1 - core)):
                target = out_ref.at[pl.ds(pl.multiple_of(where * rows, rows), rows)]
                pairs.append((source.at[:, cols], target))
        for copy in copies(pairs, sems):
            copy.wait()

    return order(
        run,
        (own, partner),
        [ANY, ANY],
        [jax.ShapeDtypeStruct((2 * rows, piece), jnp.bfloat16)] * HALVES,
        [pltpu.SemaphoreType.DMA((2 * HALVES,))],
        4,
        after,
    )


def join_cores_across(order, own, partner, after=()):
    features, rows = own.shape

    def run(place_ref, own_ref, partner_ref, out_ref, sems):
        core = place_ref[place_ref.shape[0] - 1]
        pairs = []
        for source, where in ((own_ref, core), (partner_ref, 1 - core)):
            cols = pl.ds(pl.multiple_of(where * rows, rows), rows)
            pairs.append((source, out_ref.at[:, cols]))
        for copy in copies(pairs, sems):
            copy.wait()

    return order(
        run,
        (own, partner),
        [ANY, ANY],
        [jax.ShapeDtypeStruct((features, 2 * rows), jnp.bfloat16)],
        [pltpu.SemaphoreType.DMA((2,))],
        4,
        after,
    )[0]


def assemble(order, pieces, others, across, after=()):
    chips, parts = len(pieces), len(pieces[0])
    first, second = pieces[0][0].shape
    shape = (first * parts, second * chips) if across else (first * chips, second * parts)

    def run(place_ref, *refs):
        piece_refs = [refs[p * parts : (p + 1) * parts] for p in range(chips)]
        rest = refs[chips * parts :]
        other_refs = [rest[p * parts : (p + 1) * parts] for p in range(chips - 1)]
        out_ref, sems = rest[(chips - 1) * parts :]
        position = place_ref[chips]

        def pairs(p, source):
            for j in range(parts):
                if across:
                    at = pl.ds(pl.multiple_of(place_ref[p] * second, second), second)
                    target = out_ref.at[pl.ds(j * first, first), at]
                else:
                    at = pl.ds(pl.multiple_of(place_ref[p] * first, first), first)
                    target = out_ref.at[at, pl.ds(j * second, second)]
                yield pltpu.make_async_copy(source[j], target, sems.at[p * parts + j])

        def begin(p, source):
            for copy in pairs(p, source):
                copy.start()

        begin(0, piece_refs[0])
        for p in range(1, chips):
            pl.when(position >= p)(lambda p=p: begin(p, piece_refs[p]))
            pl.when(position < p)(lambda p=p: begin(p, other_refs[chips - p - 1]))
        for p in range(chips):
            for copy in pairs(p, piece_refs[0]):
                copy.wait()

    arrays = [part for shard in (*pieces, *others) for part in shard]
    return order(
        run,
        tuple(arrays),
        [ANY] * len(arrays),
        [jax.ShapeDtypeStruct(shape, jnp.bfloat16)],
        [pltpu.SemaphoreType.DMA((chips * parts,))],
        4,
        after,
    )[0]


def nesterov(delta, base_part, momentum_part):
    momentum_next = 0.9 * momentum_part + delta
    base_next = (base_part.astype(jnp.float32) - 0.7 * (delta + 0.9 * momentum_next)).astype(
        jnp.bfloat16
    )
    return (base_next, momentum_next)


def per_device(
    tokens,
    norm_gain,
    value_weight,
    output_weight,
    out_cotangent,
    base_params,
    outer_momentum,
    delta_values,
    delta_exponents,
):
    replicas = lax.axis_size("replica")
    devices = lax.axis_size("fsdp")
    chips = devices // 2
    me = lax.axis_index("fsdp")
    chip, core = me // 2, me % 2
    position = jnp.where(core == 0, chip, chips - 1 - chip)
    steps = jnp.arange(chips, dtype=jnp.int32)
    behind = jnp.where(core == 0, chip - steps + chips, chip + steps) % chips
    order = Order(jnp.concatenate([behind, position[None], core[None]]).astype(jnp.int32))
    shard = value_weight.shape[1]
    block = 2 * shard
    cotangent = out_cotangent[0]
    bf16, f32 = jnp.bfloat16, jnp.float32

    def swap(value):
        return lax.ppermute(value, "fsdp", [(i, i ^ 1) for i in range(devices)])

    def move(value, active=lambda y: True):
        return lax.ppermute(value, "fsdp", move_perm(chips, active))

    class Gradient:
        def __init__(self, mid, x):
            terms = lax.dot_general(mid, x, (((0,), (0,)), ((), ())), preferred_element_type=f32)
            self.terms = terms.astype(bf16)
            self.across = [None] + [swap(self.block(behind[chips - s])) for s in range(1, chips)]
            self.arrived = None

        def block(self, where):
            return lax.dynamic_slice_in_dim(self.terms, where * block, block, 1)

        def message(self, step):
            term = self.block(behind[step]).astype(f32) + self.across[step].astype(f32)
            if self.arrived is not None:
                term = term + self.arrived.astype(f32)
            return term.astype(bf16)

        def reduce(self, step):
            message = self.message(step)
            self.arrived = move(message, lambda y: y <= step - 1)
            return message

        def finish(self):
            whole = self.block(chip).astype(f32) + self.arrived.astype(f32)
            mine = lax.dynamic_slice_in_dim(whole, core * shard, shard, 1)
            partners = lax.dynamic_slice_in_dim(whole, (1 - core) * shard, shard, 1)
            return (mine + swap(partners.astype(bf16)).astype(f32)).T

    first_own, second_own = value_weight[0], output_weight[0].T
    first_partner, second_partner = swap(first_own), swap(second_own)

    along = list(join_cores(order, first_own, first_partner, (second_partner,)))
    pieces, others = [list(along)], []
    normed = normalise(order, tokens[0], norm_gain)
    for step in range(1, chips):
        along = [move(part, lambda y: y >= step - 1) for part in along]
        if step == 1:
            along = [fence(order, along[0])[0], *along[1:]]
        pieces.append(list(along))
        others.append([swap(part) for part in along])
    weight = assemble(order, pieces, others, False)
    values = jnp.dot(normed, weight, preferred_element_type=f32).astype(bf16)

    message = join_cores_across(order, second_own, second_partner, (pieces[-1][0],))
    arrived = move(message)
    values = fence(order, values, after=(arrived,))[0]
    first = Gradient(values, cotangent)
    pieces, others = [[message]], []
    for step in range(1, chips):
        pieces.append([arrived])
        others.append([swap(arrived)])
        first.arrived = arrived
        message = jnp.where(position >= step, arrived, first.message(step))
        arrived = move(message)
    first.arrived = arrived
    weight = assemble(order, pieces, others, True, (message,))

    half = weight.shape[0] // HALVES
    second = []
    for j in range(HALVES):
        part = weight[j * half : (j + 1) * half]
        mid = lax.dot_general(
            cotangent, part, (((1,), (1,)), ((), ())), preferred_element_type=f32
        ).astype(bf16)
        if j == HALVES - 1:
            mid = fence(order, mid, after=(arrived,))[0]
        second.append(Gradient(mid, normed))
    for step in range(1, chips):
        for gradient in second:
            gradient.reduce(step)
    output_grad = first.finish()

    bits = replicas.bit_length() - 1
    if replicas != 1 << bits or bits < 1:
        raise ValueError("replicas")
    half = base_params.shape[0] // 2
    sums = []
    for index in range(2):
        rows = slice(index * half, (index + 1) * half)
        scale = jnp.exp2(delta_exponents[0, rows].astype(f32))[:, None]
        total = delta_values[0, rows].astype(f32) * scale
        for turn in range(bits):
            mine = total.astype(bf16)
            bit = 1 << ((turn + index) % bits)
            theirs = lax.ppermute(mine, "replica", [(i, i ^ bit) for i in range(replicas)])
            total = mine.astype(f32) + theirs.astype(f32)
        sums.append(total)
    delta = jnp.concatenate(sums) * (1.0 / replicas)
    new_base, new_momentum = nesterov(delta, base_params, outer_momentum)
    value_grad = jnp.concatenate([gradient.finish() for gradient in second], axis=1)
    return (value_grad[None], output_grad[None], new_base, new_momentum)


def solution(mesh):
    return jax.shard_map(
        per_device,
        mesh=mesh,
        in_specs=(
            P("replica", "fsdp", None),
            P(),
            P("replica", "fsdp", None),
            P("replica", "fsdp", None),
            P("replica", "fsdp", None),
            P("fsdp", None),
            P("fsdp", None),
            P("replica", "fsdp", None),
            P("replica", "fsdp"),
        ),
        out_specs=(
            P("replica", "fsdp", None),
            P("replica", "fsdp", None),
            P("fsdp", None),
            P("fsdp", None),
        ),
        check_vma=False,
    )
```

```python
import jax
import jax.numpy as jnp
from jax import lax
from jax.experimental import pallas as pl
from jax.experimental.pallas import tpu as pltpu
from jax.sharding import PartitionSpec as P

HALVES = 2
ROW_TILE = 128
FLOPS_PER_US = 10**9
ANY = pl.BlockSpec(memory_space=pl.ANY)


def move_perm(chips, active):
    pairs = []
    for z in range(chips):
        if z < chips - 1 and active(z):
            pairs.append((2 * z, 2 * z + 2))
        if z > 0 and active(chips - 1 - z):
            pairs.append((2 * z + 1, 2 * z - 1))
    return pairs


class Order:
    def __init__(self, place):
        self.place = place
        self.last = ()

    def __call__(
        self, kernel, args, in_specs, out_shape, scratch, vmem, after=(), aliases=None, grid=1,
        out_specs=None, us=1.0,
    ):
        after = self.last + tuple(after)
        count = len(args)

        def ordered(place_ref, *refs):
            kernel(place_ref, *refs[:count], *refs[count + len(after) :])

        result = pl.pallas_call(
            ordered,
            grid_spec=pltpu.PrefetchScalarGridSpec(
                num_scalar_prefetch=1,
                grid=(grid,),
                in_specs=in_specs + [ANY] * len(after),
                out_specs=out_specs or [ANY] * len(out_shape),
                scratch_shapes=scratch,
            ),
            out_shape=out_shape,
            input_output_aliases={1 + i: o for i, o in (aliases or {}).items()},
            compiler_params=pltpu.CompilerParams(vmem_limit_bytes=vmem * 1024 * 1024),
            cost_estimate=pl.CostEstimate(flops=int(us * FLOPS_PER_US), bytes_accessed=1, transcendentals=0),
            name=kernel.__qualname__.split(".")[0],
        )(self.place, *args, *after)
        self.last = (result[0],)
        return result


def copies(pairs, sems):
    started = [pltpu.make_async_copy(a, b, sems.at[i]) for i, (a, b) in enumerate(pairs)]
    for copy in started:
        copy.start()
    return started


def fence(order, *values, after=()):
    def fence(*refs):
        pass

    shapes = [jax.ShapeDtypeStruct(v.shape, v.dtype) for v in values]
    aliases = {i: i for i in range(len(values))}
    return order(fence, values, [ANY] * len(values), shapes, [], 4, after, aliases)


def normalise(order, tokens, gain, after=()):
    rows, model = tokens.shape

    def run(_, tokens_ref, gain_ref, out_ref):
        xf = tokens_ref[...].astype(jnp.float32)
        scale = lax.rsqrt(jnp.mean(xf * xf, axis=1, keepdims=True) + 1e-05)
        out_ref[...] = (xf * scale * gain_ref[...]).astype(jnp.bfloat16)

    tile = pl.BlockSpec((ROW_TILE, model), lambda i, _: (i, 0))
    return order(
        run,
        (tokens, gain[None]),
        [tile, pl.BlockSpec((1, model), lambda i, _: (0, 0))],
        [jax.ShapeDtypeStruct((rows, model), jnp.bfloat16)],
        [],
        16,
        after,
        grid=rows // ROW_TILE,
        out_specs=[tile],
        us=20.0,
    )[0]


def join_cores(order, own, partner, parts, after=()):
    rows, features = own.shape
    piece = features // parts

    def run(place_ref, own_ref, partner_ref, *refs):
        out_refs, sems = refs[:parts], refs[parts]
        core = place_ref[place_ref.shape[0] - 1]
        pairs = []
        for j, out_ref in enumerate(out_refs):
            cols = pl.ds(j * piece, piece)
            for source, where in ((own_ref, core), (partner_ref, 1 - core)):
                target = out_ref.at[pl.ds(pl.multiple_of(where * rows, rows), rows)]
                pairs.append((source.at[:, cols], target))
        for copy in copies(pairs, sems):
            copy.wait()

    return order(
        run,
        (own, partner),
        [ANY, ANY],
        [jax.ShapeDtypeStruct((2 * rows, piece), jnp.bfloat16)] * parts,
        [pltpu.SemaphoreType.DMA((2 * parts,))],
        4,
        after,
    )


def assemble(order, pieces, others, parts, after=()):
    chips, held = len(pieces), len(pieces[0])
    block, width = pieces[0][0].shape
    features = held * width
    count = max(parts, held)
    piece = features // count
    wide = features // parts

    def run(place_ref, *refs):
        piece_refs = [refs[p * held : (p + 1) * held] for p in range(chips)]
        rest = refs[chips * held :]
        other_refs = [rest[p * held : (p + 1) * held] for p in range(chips - 1)]
        out_refs, sems = rest[(chips - 1) * held : -1], rest[-1]
        position = place_ref[chips]

        def moves(p, source):
            rows = pl.ds(pl.multiple_of(place_ref[p] * block, block), block)
            for j in range(count):
                at = j * piece
                taken = source[at // width].at[:, pl.ds(at % width, piece)]
                target = out_refs[at // wide].at[rows, pl.ds(at % wide, piece)]
                yield pltpu.make_async_copy(taken, target, sems.at[p * count + j])

        def begin(p, source):
            for copy in moves(p, source):
                copy.start()

        begin(0, piece_refs[0])
        for p in range(1, chips):
            pl.when(position >= p)(lambda p=p: begin(p, piece_refs[p]))
            pl.when(position < p)(lambda p=p: begin(p, other_refs[chips - p - 1]))
        for p in range(chips):
            for copy in moves(p, piece_refs[0]):
                copy.wait()

    arrays = [part for shard in (*pieces, *others) for part in shard]
    return order(
        run,
        tuple(arrays),
        [ANY] * len(arrays),
        [jax.ShapeDtypeStruct((chips * block, wide), jnp.bfloat16)] * parts,
        [pltpu.SemaphoreType.DMA((chips * count,))],
        4,
        after,
        us=2.4,
    )


def nesterov(delta, base_part, momentum_part):
    momentum_next = 0.9 * momentum_part + delta
    base_next = (base_part.astype(jnp.float32) - 0.7 * (delta + 0.9 * momentum_next)).astype(
        jnp.bfloat16
    )
    return (base_next, momentum_next)


def per_device(
    tokens,
    norm_gain,
    value_weight,
    output_weight,
    out_cotangent,
    base_params,
    outer_momentum,
    delta_values,
    delta_exponents,
):
    replicas = lax.axis_size("replica")
    devices = lax.axis_size("fsdp")
    chips = devices // 2
    me = lax.axis_index("fsdp")
    chip, core = me // 2, me % 2
    position = jnp.where(core == 0, chip, chips - 1 - chip)
    steps = jnp.arange(chips, dtype=jnp.int32)
    behind = jnp.where(core == 0, chip - steps + chips, chip + steps) % chips
    order = Order(jnp.concatenate([behind, position[None], core[None]]).astype(jnp.int32))
    shard = value_weight.shape[1]
    block = 2 * shard
    cotangent = out_cotangent[0]
    bf16, f32 = jnp.bfloat16, jnp.float32

    def swap(value):
        return lax.ppermute(value, "fsdp", [(i, i ^ 1) for i in range(devices)])

    def move(value, active=lambda y: True):
        return lax.ppermute(value, "fsdp", move_perm(chips, active))

    class Gradient:
        def __init__(self, mid, x, after=()):
            terms = lax.dot_general(mid, x, (((0,), (0,)), ((), ())), preferred_element_type=f32)
            self.terms = terms.astype(bf16)
            if after:
                self.terms = fence(order, self.terms, after=after)[0]
            self.across = [None] + [swap(self.block(behind[chips - s])) for s in range(1, chips)]
            self.arrived = None

        def block(self, where):
            return lax.dynamic_slice_in_dim(self.terms, where * block, block, 1)

        def message(self, step):
            term = self.block(behind[step]).astype(f32) + self.across[step].astype(f32)
            if self.arrived is not None:
                term = term + self.arrived.astype(f32)
            return term.astype(bf16)

        def reduce(self, step):
            message = self.message(step)
            self.arrived = move(message, lambda y: y <= step - 1)
            return message

        def finish(self):
            whole = self.block(chip).astype(f32) + self.arrived.astype(f32)
            mine = lax.dynamic_slice_in_dim(whole, core * shard, shard, 1)
            partners = lax.dynamic_slice_in_dim(whole, (1 - core) * shard, shard, 1)
            return (mine + swap(partners.astype(bf16)).astype(f32)).T

    def gather(own):
        along = list(own)
        pieces, others = [list(along)], []
        for step in range(1, chips):
            along = [move(part, lambda y: y >= step - 1) for part in along]
            pieces.append(list(along))
            others.append([swap(part) for part in along])
        return pieces, others

    first_own, second_own = value_weight[0], output_weight[0]
    first_partner, second_partner = swap(first_own), swap(second_own)

    joined = join_cores(order, first_own, first_partner, HALVES, (second_partner,))
    normed = normalise(order, tokens[0], norm_gain, ())
    pieces, others = gather(joined)
    early = pieces[-1]

    joined = join_cores(order, second_own, second_partner, 1, (early[0],))
    weight = assemble(order, pieces, others, 1, ())[0]
    values = jnp.dot(normed, weight, preferred_element_type=f32).astype(bf16)
    pieces, others = gather(joined)
    values = fence(order, values, after=(pieces[1][0],))[0]
    first = Gradient(values, cotangent, (pieces[2][0],))
    sent = [first.reduce(step) for step in range(1, chips)]

    parts = assemble(order, pieces, others, HALVES, (sent[1],))
    second = []
    for part in parts:
        mid = jnp.dot(cotangent, part, preferred_element_type=f32).astype(bf16)
        if part is parts[-1]:
            mid = fence(order, mid, after=(sent[-1],))[0]
        second.append(Gradient(mid, normed))
    for step in range(1, chips):
        for gradient in second:
            gradient.reduce(step)
    output_grad = first.finish()

    bits = replicas.bit_length() - 1
    if replicas != 1 << bits or bits < 1:
        raise ValueError("replicas")
    half = base_params.shape[0] // 2
    sums = []
    for index in range(2):
        rows = slice(index * half, (index + 1) * half)
        scale = jnp.exp2(delta_exponents[0, rows].astype(f32))[:, None]
        total = delta_values[0, rows].astype(f32) * scale
        for turn in range(bits):
            mine = total.astype(bf16)
            bit = 1 << ((turn + index) % bits)
            theirs = lax.ppermute(mine, "replica", [(i, i ^ bit) for i in range(replicas)])
            total = lax.optimization_barrier(mine).astype(f32) + theirs.astype(f32)
        sums.append(total)
    delta = jnp.concatenate(sums) * (1.0 / replicas)
    new_base, new_momentum = nesterov(delta, base_params, outer_momentum)
    value_grad = jnp.concatenate([gradient.finish() for gradient in second], axis=1)
    return (value_grad[None], output_grad[None], new_base, new_momentum)


def solution(mesh):
    return jax.shard_map(
        per_device,
        mesh=mesh,
        in_specs=(
            P("replica", "fsdp", None),
            P(),
            P("replica", "fsdp", None),
            P("replica", "fsdp", None),
            P("replica", "fsdp", None),
            P("fsdp", None),
            P("fsdp", None),
            P("replica", "fsdp", None),
            P("replica", "fsdp"),
        ),
        out_specs=(
            P("replica", "fsdp", None),
            P("replica", "fsdp", None),
            P("fsdp", None),
            P("fsdp", None),
        ),
        check_vma=False,
    )
```

```python
import jax
import jax.numpy as jnp
from jax import lax
from jax.experimental import pallas as pl
from jax.experimental.pallas import tpu as pltpu
from jax.sharding import PartitionSpec as P

HALVES = 2
ROW_TILE = 128
FLOPS_PER_US = 10**9
ANY = pl.BlockSpec(memory_space=pl.ANY)


def move_perm(chips, active):
    pairs = []
    for z in range(chips):
        if z < chips - 1 and active(z):
            pairs.append((2 * z, 2 * z + 2))
        if z > 0 and active(chips - 1 - z):
            pairs.append((2 * z + 1, 2 * z - 1))
    return pairs


class Order:
    def __init__(self, place):
        self.place = place
        self.last = ()

    def __call__(
        self, kernel, args, in_specs, out_shape, scratch, vmem, after=(), aliases=None, grid=1,
        out_specs=None, us=1.0,
    ):
        after = self.last + tuple(after)
        count = len(args)

        def ordered(place_ref, *refs):
            kernel(place_ref, *refs[:count], *refs[count + len(after) :])

        result = pl.pallas_call(
            ordered,
            grid_spec=pltpu.PrefetchScalarGridSpec(
                num_scalar_prefetch=1,
                grid=(grid,),
                in_specs=in_specs + [ANY] * len(after),
                out_specs=out_specs or [ANY] * len(out_shape),
                scratch_shapes=scratch,
            ),
            out_shape=out_shape,
            input_output_aliases={1 + i: o for i, o in (aliases or {}).items()},
            compiler_params=pltpu.CompilerParams(vmem_limit_bytes=vmem * 1024 * 1024),
            cost_estimate=pl.CostEstimate(flops=int(us * FLOPS_PER_US), bytes_accessed=1, transcendentals=0),
            name=kernel.__qualname__.split(".")[0],
        )(self.place, *args, *after)
        self.last = (result[0],)
        return result


def copies(pairs, sems):
    started = [pltpu.make_async_copy(a, b, sems.at[i]) for i, (a, b) in enumerate(pairs)]
    for copy in started:
        copy.start()
    return started


def fence(order, *values, after=()):
    def fence(*refs):
        pass

    shapes = [jax.ShapeDtypeStruct(v.shape, v.dtype) for v in values]
    aliases = {i: i for i in range(len(values))}
    return order(fence, values, [ANY] * len(values), shapes, [], 4, after, aliases)


def normalise(order, tokens, gain, after=()):
    rows, model = tokens.shape

    def run(_, tokens_ref, gain_ref, out_ref):
        xf = tokens_ref[...].astype(jnp.float32)
        scale = lax.rsqrt(jnp.mean(xf * xf, axis=1, keepdims=True) + 1e-05)
        out_ref[...] = (xf * scale * gain_ref[...]).astype(jnp.bfloat16)

    tile = pl.BlockSpec((ROW_TILE, model), lambda i, _: (i, 0))
    return order(
        run,
        (tokens, gain[None]),
        [tile, pl.BlockSpec((1, model), lambda i, _: (0, 0))],
        [jax.ShapeDtypeStruct((rows, model), jnp.bfloat16)],
        [],
        16,
        after,
        grid=rows // ROW_TILE,
        out_specs=[tile],
        us=20.0,
    )[0]


def join_cores(order, own, partner, parts, after=()):
    rows, features = own.shape
    piece = features // parts

    def run(place_ref, own_ref, partner_ref, *refs):
        out_refs, sems = refs[:parts], refs[parts]
        core = place_ref[place_ref.shape[0] - 1]
        pairs = []
        for j, out_ref in enumerate(out_refs):
            cols = pl.ds(j * piece, piece)
            for source, where in ((own_ref, core), (partner_ref, 1 - core)):
                target = out_ref.at[pl.ds(pl.multiple_of(where * rows, rows), rows)]
                pairs.append((source.at[:, cols], target))
        for copy in copies(pairs, sems):
            copy.wait()

    return order(
        run,
        (own, partner),
        [ANY, ANY],
        [jax.ShapeDtypeStruct((2 * rows, piece), jnp.bfloat16)] * parts,
        [pltpu.SemaphoreType.DMA((2 * parts,))],
        4,
        after,
    )


def assemble(order, pieces, others, parts, after=()):
    chips, held = len(pieces), len(pieces[0])
    block, width = pieces[0][0].shape
    features = held * width
    count = max(parts, held)
    piece = features // count
    wide = features // parts

    def run(place_ref, *refs):
        piece_refs = [refs[p * held : (p + 1) * held] for p in range(chips)]
        rest = refs[chips * held :]
        other_refs = [rest[p * held : (p + 1) * held] for p in range(chips - 1)]
        out_refs, sems = rest[(chips - 1) * held : -1], rest[-1]
        position = place_ref[chips]

        def moves(p, source):
            rows = pl.ds(pl.multiple_of(place_ref[p] * block, block), block)
            for j in range(count):
                at = j * piece
                taken = source[at // width].at[:, pl.ds(at % width, piece)]
                target = out_refs[at // wide].at[rows, pl.ds(at % wide, piece)]
                yield pltpu.make_async_copy(taken, target, sems.at[p * count + j])

        def begin(p, source):
            for copy in moves(p, source):
                copy.start()

        begin(0, piece_refs[0])
        for p in range(1, chips):
            pl.when(position >= p)(lambda p=p: begin(p, piece_refs[p]))
            pl.when(position < p)(lambda p=p: begin(p, other_refs[chips - p - 1]))
        for p in range(chips):
            for copy in moves(p, piece_refs[0]):
                copy.wait()

    arrays = [part for shard in (*pieces, *others) for part in shard]
    return order(
        run,
        tuple(arrays),
        [ANY] * len(arrays),
        [jax.ShapeDtypeStruct((chips * block, wide), jnp.bfloat16)] * parts,
        [pltpu.SemaphoreType.DMA((chips * count,))],
        4,
        after,
        us=2.4,
    )


def nesterov(delta, base_part, momentum_part):
    momentum_next = 0.9 * momentum_part + delta
    base_next = (base_part.astype(jnp.float32) - 0.7 * (delta + 0.9 * momentum_next)).astype(
        jnp.bfloat16
    )
    return (base_next, momentum_next)


def per_device(
    tokens,
    norm_gain,
    value_weight,
    output_weight,
    out_cotangent,
    base_params,
    outer_momentum,
    delta_values,
    delta_exponents,
):
    replicas = lax.axis_size("replica")
    devices = lax.axis_size("fsdp")
    chips = devices // 2
    me = lax.axis_index("fsdp")
    chip, core = me // 2, me % 2
    position = jnp.where(core == 0, chip, chips - 1 - chip)
    steps = jnp.arange(chips, dtype=jnp.int32)
    behind = jnp.where(core == 0, chip - steps + chips, chip + steps) % chips
    order = Order(jnp.concatenate([behind, position[None], core[None]]).astype(jnp.int32))
    shard = value_weight.shape[1]
    block = 2 * shard
    cotangent = out_cotangent[0]
    bf16, f32 = jnp.bfloat16, jnp.float32

    def swap(value):
        return lax.ppermute(value, "fsdp", [(i, i ^ 1) for i in range(devices)])

    def move(value, active=lambda y: True):
        return lax.ppermute(value, "fsdp", move_perm(chips, active))

    class Gradient:
        def __init__(self, mid, x, after=()):
            terms = lax.dot_general(mid, x, (((0,), (0,)), ((), ())), preferred_element_type=f32)
            self.terms = terms.astype(bf16)
            if after:
                self.terms = fence(order, self.terms, after=after)[0]
            self.across = [None] + [swap(self.block(behind[chips - s])) for s in range(1, chips)]
            self.arrived = None

        def block(self, where):
            chosen = self.terms[:, :block]
            for at in range(1, chips):
                part = self.terms[:, at * block : (at + 1) * block]
                chosen = jnp.where(where == at, part, chosen)
            return chosen

        def message(self, step):
            term = self.block(behind[step]).astype(f32) + self.across[step].astype(f32)
            if self.arrived is not None:
                term = term + self.arrived.astype(f32)
            return term.astype(bf16)

        def reduce(self, step):
            message = self.message(step)
            self.arrived = move(message, lambda y: y <= step - 1)
            return message

        def finish(self):
            whole = self.block(chip).astype(f32) + self.arrived.astype(f32)
            first, second = whole[:, :shard], whole[:, shard:]
            mine = jnp.where(core == 0, first, second)
            partners = jnp.where(core == 0, second, first)
            return (mine + swap(partners.astype(bf16)).astype(f32)).T

    def gather(own, at_first=False):
        along = list(own)
        pieces, others = [list(along)], []
        for step in range(1, chips):
            along = [move(part, lambda y: y >= step - 1) for part in along]
            if at_first and step == 1:
                along[:1] = fence(order, along[0])
            pieces.append(list(along))
            others.append([swap(part) for part in along])
        return pieces, others

    first_own, second_own = value_weight[0], output_weight[0]
    first_partner, second_partner = swap(first_own), swap(second_own)

    bits = replicas.bit_length() - 1
    if replicas != 1 << bits or bits < 1:
        raise ValueError("replicas")
    rows_half = base_params.shape[0] // 2
    sums, early = [], []
    for index in range(2):
        rows = slice(index * rows_half, (index + 1) * rows_half)
        scale = jnp.exp2(delta_exponents[0, rows].astype(f32))[:, None]
        total = delta_values[0, rows].astype(f32) * scale
        for turn in range(bits):
            mine = total.astype(bf16)
            bit = 1 << ((turn + index) % bits)
            theirs = lax.ppermute(mine, "replica", [(i, i ^ bit) for i in range(replicas)])
            if turn == 0:
                early.append(theirs)
            total = lax.optimization_barrier(mine).astype(f32) + theirs.astype(f32)
        sums.append(total)

    joined = join_cores(order, first_own, first_partner, HALVES, (second_partner,))
    normed = normalise(order, tokens[0], norm_gain, ())
    pieces, others = gather(joined, at_first=True)
    last = pieces[-1]

    joined = join_cores(order, second_own, second_partner, 1, (last[0],))
    weight = assemble(order, pieces, others, 1, early)[0]
    values = jnp.dot(normed, weight, preferred_element_type=f32).astype(bf16)
    pieces, others = gather(joined)
    values = fence(order, values, after=(pieces[1][0],))[0]
    first = Gradient(values, cotangent, (pieces[2][0],))
    sent = [first.reduce(step) for step in range(1, chips)]

    weight = assemble(order, pieces, others, 1, (sent[1],))[0]
    mid = jnp.dot(cotangent, weight, preferred_element_type=f32).astype(bf16)
    mid = fence(order, mid, after=(sent[-1],))[0]
    half = mid.shape[1] // HALVES
    second = [Gradient(mid[:, j * half : (j + 1) * half], normed) for j in range(HALVES)]
    for step in range(1, chips):
        for gradient in second:
            gradient.reduce(step)
    output_grad = first.finish()

    delta = jnp.concatenate(sums) * (1.0 / replicas)
    new_base, new_momentum = nesterov(delta, base_params, outer_momentum)
    value_grad = jnp.concatenate([gradient.finish() for gradient in second], axis=1)
    return (value_grad[None], output_grad[None], new_base, new_momentum)


def solution(mesh):
    return jax.shard_map(
        per_device,
        mesh=mesh,
        in_specs=(
            P("replica", "fsdp", None),
            P(),
            P("replica", "fsdp", None),
            P("replica", "fsdp", None),
            P("replica", "fsdp", None),
            P("fsdp", None),
            P("fsdp", None),
            P("replica", "fsdp", None),
            P("replica", "fsdp"),
        ),
        out_specs=(
            P("replica", "fsdp", None),
            P("replica", "fsdp", None),
            P("fsdp", None),
            P("fsdp", None),
        ),
        check_vma=False,
    )
```

```python
import jax
import jax.numpy as jnp
from jax import lax
from jax.experimental import pallas as pl
from jax.experimental.pallas import tpu as pltpu
from jax.sharding import PartitionSpec as P

HALVES = 2
ROW_TILE = 128
FLOPS_PER_US = 10**9
ANY = pl.BlockSpec(memory_space=pl.ANY)


def move_perm(chips, active):
    pairs = []
    for z in range(chips):
        if z < chips - 1 and active(z):
            pairs.append((2 * z, 2 * z + 2))
        if z > 0 and active(chips - 1 - z):
            pairs.append((2 * z + 1, 2 * z - 1))
    return pairs


class Order:
    def __init__(self, place):
        self.place = place
        self.last = ()

    def __call__(
        self, kernel, args, in_specs, out_shape, scratch, vmem, after=(), aliases=None, grid=1,
        out_specs=None, us=1.0,
    ):
        after = self.last + tuple(after)
        count = len(args)

        def ordered(place_ref, *refs):
            kernel(place_ref, *refs[:count], *refs[count + len(after) :])

        result = pl.pallas_call(
            ordered,
            grid_spec=pltpu.PrefetchScalarGridSpec(
                num_scalar_prefetch=1,
                grid=(grid,),
                in_specs=in_specs + [ANY] * len(after),
                out_specs=out_specs or [ANY] * len(out_shape),
                scratch_shapes=scratch,
            ),
            out_shape=out_shape,
            input_output_aliases={1 + i: o for i, o in (aliases or {}).items()},
            compiler_params=pltpu.CompilerParams(vmem_limit_bytes=vmem * 1024 * 1024),
            cost_estimate=pl.CostEstimate(flops=int(us * FLOPS_PER_US), bytes_accessed=1, transcendentals=0),
            name=kernel.__qualname__.split(".")[0],
        )(self.place, *args, *after)
        self.last = (result[0],)
        return result


def copies(pairs, sems):
    started = [pltpu.make_async_copy(a, b, sems.at[i]) for i, (a, b) in enumerate(pairs)]
    for copy in started:
        copy.start()
    return started


def fence(order, *values, after=()):
    def fence(*refs):
        pass

    shapes = [jax.ShapeDtypeStruct(v.shape, v.dtype) for v in values]
    aliases = {i: i for i in range(len(values))}
    return order(fence, values, [ANY] * len(values), shapes, [], 4, after, aliases)


def normalise(order, tokens, gain, after=()):
    rows, model = tokens.shape

    def run(_, tokens_ref, gain_ref, out_ref):
        xf = tokens_ref[...].astype(jnp.float32)
        scale = lax.rsqrt(jnp.mean(xf * xf, axis=1, keepdims=True) + 1e-05)
        out_ref[...] = (xf * scale * gain_ref[...]).astype(jnp.bfloat16)

    tile = pl.BlockSpec((ROW_TILE, model), lambda i, _: (i, 0))
    return order(
        run,
        (tokens, gain[None]),
        [tile, pl.BlockSpec((1, model), lambda i, _: (0, 0))],
        [jax.ShapeDtypeStruct((rows, model), jnp.bfloat16)],
        [],
        16,
        after,
        grid=rows // ROW_TILE,
        out_specs=[tile],
        us=20.0,
    )[0]


def join_cores(order, own, partner, parts, after=()):
    rows, features = own.shape
    piece = features // parts

    def run(place_ref, own_ref, partner_ref, *refs):
        out_refs, sems = refs[:parts], refs[parts]
        core = place_ref[place_ref.shape[0] - 1]
        pairs = []
        for j, out_ref in enumerate(out_refs):
            cols = pl.ds(j * piece, piece)
            for source, where in ((own_ref, core), (partner_ref, 1 - core)):
                target = out_ref.at[pl.ds(pl.multiple_of(where * rows, rows), rows)]
                pairs.append((source.at[:, cols], target))
        for copy in copies(pairs, sems):
            copy.wait()

    return order(
        run,
        (own, partner),
        [ANY, ANY],
        [jax.ShapeDtypeStruct((2 * rows, piece), jnp.bfloat16)] * parts,
        [pltpu.SemaphoreType.DMA((2 * parts,))],
        4,
        after,
    )


def assemble(order, pieces, others, parts, after=()):
    chips, held = len(pieces), len(pieces[0])
    block, width = pieces[0][0].shape
    features = held * width
    count = max(parts, held)
    piece = features // count
    wide = features // parts

    def run(place_ref, *refs):
        piece_refs = [refs[p * held : (p + 1) * held] for p in range(chips)]
        rest = refs[chips * held :]
        other_refs = [rest[p * held : (p + 1) * held] for p in range(chips - 1)]
        out_refs, sems = rest[(chips - 1) * held : -1], rest[-1]
        position = place_ref[chips]

        def moves(p, source):
            rows = pl.ds(pl.multiple_of(place_ref[p] * block, block), block)
            for j in range(count):
                at = j * piece
                taken = source[at // width].at[:, pl.ds(at % width, piece)]
                target = out_refs[at // wide].at[rows, pl.ds(at % wide, piece)]
                yield pltpu.make_async_copy(taken, target, sems.at[p * count + j])

        def begin(p, source):
            for copy in moves(p, source):
                copy.start()

        begin(0, piece_refs[0])
        for p in range(1, chips):
            pl.when(position >= p)(lambda p=p: begin(p, piece_refs[p]))
            pl.when(position < p)(lambda p=p: begin(p, other_refs[chips - p - 1]))
        for p in range(chips):
            for copy in moves(p, piece_refs[0]):
                copy.wait()

    arrays = [part for shard in (*pieces, *others) for part in shard]
    return order(
        run,
        tuple(arrays),
        [ANY] * len(arrays),
        [jax.ShapeDtypeStruct((chips * block, wide), jnp.bfloat16)] * parts,
        [pltpu.SemaphoreType.DMA((chips * count,))],
        4,
        after,
        us=2.4,
    )


def nesterov(delta, base_part, momentum_part):
    momentum_next = 0.9 * momentum_part + delta
    base_next = (base_part.astype(jnp.float32) - 0.7 * (delta + 0.9 * momentum_next)).astype(
        jnp.bfloat16
    )
    return (base_next, momentum_next)


def per_device(
    tokens,
    norm_gain,
    value_weight,
    output_weight,
    out_cotangent,
    base_params,
    outer_momentum,
    delta_values,
    delta_exponents,
):
    replicas = lax.axis_size("replica")
    devices = lax.axis_size("fsdp")
    chips = devices // 2
    me = lax.axis_index("fsdp")
    chip, core = me // 2, me % 2
    position = chip + core * (chips - 1 - 2 * chip)
    way = 1 - 2 * core
    behind = [(chip - way * s + chips) % chips for s in range(chips)]
    order = Order(jnp.stack([*behind, position, core]).astype(jnp.int32))
    shard = value_weight.shape[1]
    block = 2 * shard
    cotangent = out_cotangent[0]
    bf16, f32 = jnp.bfloat16, jnp.float32

    def swap(value):
        return lax.ppermute(value, "fsdp", [(i, i ^ 1) for i in range(devices)])

    def move(value, active=lambda y: True):
        return lax.ppermute(value, "fsdp", move_perm(chips, active))

    class Gradient:
        def __init__(self, mid, x, after=()):
            terms = lax.dot_general(mid, x, (((0,), (0,)), ((), ())), preferred_element_type=f32)
            self.terms = terms.astype(bf16)
            if after:
                self.terms = fence(order, self.terms, after=after)[0]
            self.across = [None] + [swap(self.block(behind[chips - s])) for s in range(1, chips)]
            self.arrived = None

        def block(self, where):
            chosen = self.terms[:, :block]
            for at in range(1, chips):
                part = self.terms[:, at * block : (at + 1) * block]
                chosen = jnp.where(where == at, part, chosen)
            return chosen

        def message(self, step):
            term = self.block(behind[step]).astype(f32) + self.across[step].astype(f32)
            if self.arrived is not None:
                term = term + self.arrived.astype(f32)
            return term.astype(bf16)

        def reduce(self, step):
            message = self.message(step)
            self.arrived = move(message, lambda y: y <= step - 1)
            return message

        def finish(self):
            whole = self.block(chip).astype(f32) + self.arrived.astype(f32)
            first, second = whole[:, :shard], whole[:, shard:]
            mine = jnp.where(core == 0, first, second)
            partners = jnp.where(core == 0, second, first)
            return (mine + swap(partners.astype(bf16)).astype(f32)).T

    def gather(own, at_first=False):
        along = list(own)
        pieces, others = [list(along)], []
        for step in range(1, chips):
            along = [move(part, lambda y: y >= step - 1) for part in along]
            if at_first and step == 1:
                along[:1] = fence(order, along[0])
            pieces.append(list(along))
            others.append([swap(part) for part in along])
        return pieces, others

    first_own, second_own = value_weight[0], output_weight[0]
    first_partner, second_partner = swap(first_own), swap(second_own)

    joined = join_cores(order, first_own, first_partner, HALVES, (second_partner,))
    normed = normalise(order, tokens[0], norm_gain, ())
    exponents = fence(order, delta_exponents)[0]
    bits = replicas.bit_length() - 1
    if replicas != 1 << bits or bits < 1:
        raise ValueError("replicas")
    rows_half = base_params.shape[0] // 2
    sums, early = [], []
    for index in range(2):
        rows = slice(index * rows_half, (index + 1) * rows_half)
        scale = jnp.exp2(exponents[0, rows].astype(f32))[:, None]
        total = delta_values[0, rows].astype(f32) * scale
        for turn in range(bits):
            mine = total.astype(bf16)
            bit = 1 << ((turn + index) % bits)
            theirs = lax.ppermute(mine, "replica", [(i, i ^ bit) for i in range(replicas)])
            if turn == 0:
                early.append(theirs)
            total = mine.astype(f32) + theirs.astype(f32)
        sums.append((mine, theirs))
    pieces, others = gather(joined, at_first=True)
    last = pieces[-1]

    joined = join_cores(order, second_own, second_partner, 1, (last[0],))
    weight = assemble(order, pieces, others, 1, early)[0]
    values = jnp.dot(normed, weight, preferred_element_type=f32).astype(bf16)
    pieces, others = gather(joined)
    values = fence(order, values, after=(pieces[1][0],))[0]
    first = Gradient(values, cotangent, (pieces[2][0],))
    sent = [first.reduce(step) for step in range(1, chips)]

    weight = assemble(order, pieces, others, 1, (sent[1],))[0]
    mid = jnp.dot(cotangent, weight, preferred_element_type=f32).astype(bf16)
    mid = fence(order, mid, after=(sent[-1],))[0]
    half = mid.shape[1] // HALVES
    second = [Gradient(mid[:, j * half : (j + 1) * half], normed) for j in range(HALVES)]
    for step in range(1, chips):
        sent = tuple(gradient.reduce(step) for gradient in second)
        if step == 1:
            theirs = fence(order, *(pair[1] for pair in sums), after=sent)
    output_grad = first.finish()

    total = [a.astype(f32) + b.astype(f32) for (a, _), b in zip(sums, theirs)]
    delta = jnp.concatenate(total) * (1.0 / replicas)
    new_base, new_momentum = nesterov(delta, base_params, outer_momentum)
    value_grad = jnp.concatenate([gradient.finish() for gradient in second], axis=1)
    return (value_grad[None], output_grad[None], new_base, new_momentum)


def solution(mesh):
    return jax.shard_map(
        per_device,
        mesh=mesh,
        in_specs=(
            P("replica", "fsdp", None),
            P(),
            P("replica", "fsdp", None),
            P("replica", "fsdp", None),
            P("replica", "fsdp", None),
            P("fsdp", None),
            P("fsdp", None),
            P("replica", "fsdp", None),
            P("replica", "fsdp"),
        ),
        out_specs=(
            P("replica", "fsdp", None),
            P("replica", "fsdp", None),
            P("fsdp", None),
            P("fsdp", None),
        ),
        check_vma=False,
    )
```

```python
import jax
import jax.numpy as jnp
from jax import lax
from jax.experimental import pallas as pl
from jax.experimental.pallas import tpu as pltpu
from jax.sharding import PartitionSpec as P

HALVES = 2
ROW_TILE = 128
FLOPS_PER_US = 10**9
ANY = pl.BlockSpec(memory_space=pl.ANY)


def move_perm(chips, active):
    pairs = []
    for z in range(chips):
        if z < chips - 1 and active(z):
            pairs.append((2 * z, 2 * z + 2))
        if z > 0 and active(chips - 1 - z):
            pairs.append((2 * z + 1, 2 * z - 1))
    return pairs


class Order:
    def __init__(self, place):
        self.place = place
        self.last = ()

    def __call__(
        self, kernel, args, in_specs, out_shape, scratch, vmem, after=(), aliases=None, grid=1,
        out_specs=None, us=1.0,
    ):
        after = self.last + tuple(after)
        count = len(args)

        def ordered(place_ref, *refs):
            kernel(place_ref, *refs[:count], *refs[count + len(after) :])

        result = pl.pallas_call(
            ordered,
            grid_spec=pltpu.PrefetchScalarGridSpec(
                num_scalar_prefetch=1,
                grid=(grid,),
                in_specs=in_specs + [ANY] * len(after),
                out_specs=out_specs or [ANY] * len(out_shape),
                scratch_shapes=scratch,
            ),
            out_shape=out_shape,
            input_output_aliases={1 + i: o for i, o in (aliases or {}).items()},
            compiler_params=pltpu.CompilerParams(vmem_limit_bytes=vmem * 1024 * 1024),
            cost_estimate=pl.CostEstimate(flops=int(us * FLOPS_PER_US), bytes_accessed=1, transcendentals=0),
            name=kernel.__qualname__.split(".")[0],
        )(self.place, *args, *after)
        self.last = (result[0],)
        return result


def copies(pairs, sems):
    started = [pltpu.make_async_copy(a, b, sems.at[i]) for i, (a, b) in enumerate(pairs)]
    for copy in started:
        copy.start()
    return started


def fence(order, *values, after=()):
    def fence(*refs):
        pass

    shapes = [jax.ShapeDtypeStruct(v.shape, v.dtype) for v in values]
    aliases = {i: i for i in range(len(values))}
    return order(fence, values, [ANY] * len(values), shapes, [], 4, after, aliases)


def prepare(order, tokens, cotangent, gain, chips, after=()):
    rows, model = tokens.shape
    block = model // chips

    def run(place_ref, tokens_ref, cot_ref, gain_ref, normed_out, cot_out):
        xf = tokens_ref[...].astype(jnp.float32)
        scale = lax.rsqrt(jnp.mean(xf * xf, axis=1, keepdims=True) + 1e-05)
        for p in range(chips):
            cols = pl.ds(pl.multiple_of(place_ref[p] * block, block), block)
            to = slice(p * block, (p + 1) * block)
            part = tokens_ref[:, cols].astype(jnp.float32)
            normed_out[:, to] = (part * scale * gain_ref[:, cols]).astype(jnp.bfloat16)
            cot_out[:, to] = cot_ref[:, cols]

    tile = pl.BlockSpec((ROW_TILE, model), lambda i, _: (i, 0))
    return order(
        run,
        (tokens, cotangent, gain[None]),
        [tile, tile, pl.BlockSpec((1, model), lambda i, _: (0, 0))],
        [jax.ShapeDtypeStruct((rows, model), jnp.bfloat16)] * 2,
        [],
        24,
        after,
        grid=rows // ROW_TILE,
        out_specs=[tile, tile],
        us=20.0,
    )


def join_cores(order, own, partner, parts, after=()):
    rows, features = own.shape
    piece = features // parts

    def run(place_ref, own_ref, partner_ref, *refs):
        out_refs, sems = refs[:parts], refs[parts]
        core = place_ref[place_ref.shape[0] - 1]
        pairs = []
        for j, out_ref in enumerate(out_refs):
            cols = pl.ds(j * piece, piece)
            for source, where in ((own_ref, core), (partner_ref, 1 - core)):
                target = out_ref.at[pl.ds(pl.multiple_of(where * rows, rows), rows)]
                pairs.append((source.at[:, cols], target))
        for copy in copies(pairs, sems):
            copy.wait()

    return order(
        run,
        (own, partner),
        [ANY, ANY],
        [jax.ShapeDtypeStruct((2 * rows, piece), jnp.bfloat16)] * parts,
        [pltpu.SemaphoreType.DMA((2 * parts,))],
        4,
        after,
    )


def nesterov(delta, base_part, momentum_part):
    momentum_next = 0.9 * momentum_part + delta
    base_next = (base_part.astype(jnp.float32) - 0.7 * (delta + 0.9 * momentum_next)).astype(
        jnp.bfloat16
    )
    return (base_next, momentum_next)


def per_device(
    tokens,
    norm_gain,
    value_weight,
    output_weight,
    out_cotangent,
    base_params,
    outer_momentum,
    delta_values,
    delta_exponents,
):
    replicas = lax.axis_size("replica")
    devices = lax.axis_size("fsdp")
    chips = devices // 2
    me = lax.axis_index("fsdp")
    chip, core = me // 2, me % 2
    position = chip + core * (chips - 1 - 2 * chip)
    way = 1 - 2 * core
    behind = [(chip - way * s + chips) % chips for s in range(chips)]
    order = Order(jnp.stack([*behind, position, core]).astype(jnp.int32))
    shard = value_weight.shape[1]
    block = 2 * shard
    bf16, f32 = jnp.bfloat16, jnp.float32

    def swap(value):
        return lax.ppermute(value, "fsdp", [(i, i ^ 1) for i in range(devices)])

    def move(value, active=lambda y: True):
        return lax.ppermute(value, "fsdp", move_perm(chips, active))

    class Gradient:
        def __init__(self, mid, x, after=()):
            terms = lax.dot_general(mid, x, (((0,), (0,)), ((), ())), preferred_element_type=f32)
            self.terms = terms.astype(bf16)
            if after:
                self.terms = fence(order, self.terms, after=after)[0]
            self.across = [None] + [swap(self.block(chips - s)) for s in range(1, chips)]
            self.arrived = None

        def block(self, place):
            return self.terms[:, place * block : (place + 1) * block]

        def message(self, step):
            term = self.block(step).astype(f32) + self.across[step].astype(f32)
            if self.arrived is not None:
                term = term + self.arrived.astype(f32)
            return term.astype(bf16)

        def reduce(self, step):
            message = self.message(step)
            self.arrived = move(message, lambda y: y <= step - 1)
            return message

        def finish(self):
            whole = self.block(0).astype(f32) + self.arrived.astype(f32)
            first, second = whole[:, :shard], whole[:, shard:]
            mine = jnp.where(core == 0, first, second)
            partners = jnp.where(core == 0, second, first)
            return (mine + swap(partners.astype(bf16)).astype(f32)).T

    def gather(own, at_first=False):
        along = list(own)
        pieces, others = [list(along)], []
        for step in range(1, chips):
            along = [move(part, lambda y: y >= step - 1) for part in along]
            if at_first and step == 1:
                along[:1] = fence(order, along[0])
            pieces.append(list(along))
            others.append([swap(part) for part in along])
        return pieces, others

    def assemble(pieces, others):
        shards = [jnp.concatenate(pieces[0], axis=1)]
        for p in range(1, chips):
            parts = zip(pieces[p], others[chips - p - 1])
            chosen = [jnp.where(position >= p, here, there) for here, there in parts]
            shards.append(jnp.concatenate(chosen, axis=1))
        return jnp.concatenate(shards, axis=0)

    first_own, second_own = value_weight[0], output_weight[0]
    first_partner, second_partner = swap(first_own), swap(second_own)

    joined = join_cores(order, first_own, first_partner, HALVES, (second_partner,))
    normed, cotangent = prepare(order, tokens[0], out_cotangent[0], norm_gain, chips)
    exponents = fence(order, delta_exponents)[0]
    bits = replicas.bit_length() - 1
    if replicas != 1 << bits or bits < 1:
        raise ValueError("replicas")
    rows_half = base_params.shape[0] // 2
    sums, early = [], []
    for index in range(2):
        rows = slice(index * rows_half, (index + 1) * rows_half)
        scale = jnp.exp2(exponents[0, rows].astype(f32))[:, None]
        total = delta_values[0, rows].astype(f32) * scale
        for turn in range(bits):
            mine = total.astype(bf16)
            bit = 1 << ((turn + index) % bits)
            theirs = lax.ppermute(mine, "replica", [(i, i ^ bit) for i in range(replicas)])
            if turn == 0:
                early.append(theirs)
            total = mine.astype(f32) + theirs.astype(f32)
        sums.append((mine, theirs))
    pieces, others = gather(joined, at_first=True)
    last = pieces[-1]

    joined = join_cores(order, second_own, second_partner, 1, (last[0],))
    weight = assemble(pieces, others)
    values = jnp.dot(normed, weight, preferred_element_type=f32).astype(bf16)
    pieces, others = gather(joined)
    values = fence(order, values, after=(pieces[1][0], *early))[0]
    first = Gradient(values, cotangent, (pieces[2][0],))
    sent = [first.reduce(step) for step in range(1, chips)]

    weight = assemble(pieces, others)
    mid = jnp.dot(cotangent, weight, preferred_element_type=f32).astype(bf16)
    mid = fence(order, mid, after=(sent[-1],))[0]
    half = mid.shape[1] // HALVES
    second = [Gradient(mid[:, j * half : (j + 1) * half], normed) for j in range(HALVES)]
    for step in range(1, chips):
        sent = tuple(gradient.reduce(step) for gradient in second)
        if step == 1:
            theirs = fence(order, *(pair[1] for pair in sums), after=sent)
    output_grad = first.finish()

    total = [a.astype(f32) + b.astype(f32) for (a, _), b in zip(sums, theirs)]
    delta = jnp.concatenate(total) * (1.0 / replicas)
    new_base, new_momentum = nesterov(delta, base_params, outer_momentum)
    value_grad = jnp.concatenate([gradient.finish() for gradient in second], axis=1)
    return (value_grad[None], output_grad[None], new_base, new_momentum)


def solution(mesh):
    return jax.shard_map(
        per_device,
        mesh=mesh,
        in_specs=(
            P("replica", "fsdp", None),
            P(),
            P("replica", "fsdp", None),
            P("replica", "fsdp", None),
            P("replica", "fsdp", None),
            P("fsdp", None),
            P("fsdp", None),
            P("replica", "fsdp", None),
            P("replica", "fsdp"),
        ),
        out_specs=(
            P("replica", "fsdp", None),
            P("replica", "fsdp", None),
            P("fsdp", None),
            P("fsdp", None),
        ),
        check_vma=False,
    )
```

```python
import jax
import jax.numpy as jnp
from jax import lax
from jax.experimental import pallas as pl
from jax.experimental.pallas import tpu as pltpu
from jax.sharding import PartitionSpec as P

HALVES = 2
ROW_TILE = 128
FLOPS_PER_US = 10**9
ANY = pl.BlockSpec(memory_space=pl.ANY)


def move_perm(chips, active):
    pairs = []
    for z in range(chips):
        if z < chips - 1 and active(z):
            pairs.append((2 * z, 2 * z + 2))
        if z > 0 and active(chips - 1 - z):
            pairs.append((2 * z + 1, 2 * z - 1))
    return pairs


class Order:
    def __init__(self, place):
        self.place = place
        self.last = ()

    def __call__(
        self, kernel, args, in_specs, out_shape, scratch, vmem, after=(), aliases=None, grid=1,
        out_specs=None, us=1.0,
    ):
        after = self.last + tuple(after)
        count = len(args)

        def ordered(place_ref, *refs):
            kernel(place_ref, *refs[:count], *refs[count + len(after) :])

        result = pl.pallas_call(
            ordered,
            grid_spec=pltpu.PrefetchScalarGridSpec(
                num_scalar_prefetch=1,
                grid=(grid,),
                in_specs=in_specs + [ANY] * len(after),
                out_specs=out_specs or [ANY] * len(out_shape),
                scratch_shapes=scratch,
            ),
            out_shape=out_shape,
            input_output_aliases={1 + i: o for i, o in (aliases or {}).items()},
            compiler_params=pltpu.CompilerParams(vmem_limit_bytes=vmem * 1024 * 1024),
            cost_estimate=pl.CostEstimate(flops=int(us * FLOPS_PER_US), bytes_accessed=1, transcendentals=0),
            name=kernel.__qualname__.split(".")[0],
        )(self.place, *args, *after)
        self.last = (result[0],)
        return result


def copies(pairs, sems):
    started = [pltpu.make_async_copy(a, b, sems.at[i]) for i, (a, b) in enumerate(pairs)]
    for copy in started:
        copy.start()
    return started


def fence(order, *values, after=()):
    def fence(*refs):
        pass

    shapes = [jax.ShapeDtypeStruct(v.shape, v.dtype) for v in values]
    aliases = {i: i for i in range(len(values))}
    return order(fence, values, [ANY] * len(values), shapes, [], 4, after, aliases)


def prepare(order, tokens, cotangent, gain, chips, after=()):
    rows, model = tokens.shape
    block = model // chips

    def run(place_ref, tokens_ref, cot_ref, gain_ref, normed_out, cot_out):
        xf = tokens_ref[...].astype(jnp.float32)
        scale = lax.rsqrt(jnp.mean(xf * xf, axis=1, keepdims=True) + 1e-05)
        for p in range(chips):
            cols = pl.ds(pl.multiple_of(place_ref[p] * block, block), block)
            to = slice(p * block, (p + 1) * block)
            part = tokens_ref[:, cols].astype(jnp.float32)
            normed_out[:, to] = (part * scale * gain_ref[:, cols]).astype(jnp.bfloat16)
            cot_out[:, to] = cot_ref[:, cols]

    tile = pl.BlockSpec((ROW_TILE, model), lambda i, _: (i, 0))
    return order(
        run,
        (tokens, cotangent, gain[None]),
        [tile, tile, pl.BlockSpec((1, model), lambda i, _: (0, 0))],
        [jax.ShapeDtypeStruct((rows, model), jnp.bfloat16)] * 2,
        [],
        24,
        after,
        grid=rows // ROW_TILE,
        out_specs=[tile, tile],
        us=20.0,
    )


def join_cores(order, own, partner, parts, after=()):
    rows, features = own.shape
    piece = features // parts

    def run(place_ref, own_ref, partner_ref, *refs):
        out_refs, sems = refs[:parts], refs[parts]
        core = place_ref[place_ref.shape[0] - 1]
        pairs = []
        for j, out_ref in enumerate(out_refs):
            cols = pl.ds(j * piece, piece)
            for source, where in ((own_ref, core), (partner_ref, 1 - core)):
                target = out_ref.at[pl.ds(pl.multiple_of(where * rows, rows), rows)]
                pairs.append((source.at[:, cols], target))
        for copy in copies(pairs, sems):
            copy.wait()

    return order(
        run,
        (own, partner),
        [ANY, ANY],
        [jax.ShapeDtypeStruct((2 * rows, piece), jnp.bfloat16)] * parts,
        [pltpu.SemaphoreType.DMA((2 * parts,))],
        4,
        after,
    )


def nesterov(delta, base_part, momentum_part):
    momentum_next = 0.9 * momentum_part + delta
    base_next = (base_part.astype(jnp.float32) - 0.7 * (delta + 0.9 * momentum_next)).astype(
        jnp.bfloat16
    )
    return (base_next, momentum_next)


def per_device(
    tokens,
    norm_gain,
    value_weight,
    output_weight,
    out_cotangent,
    base_params,
    outer_momentum,
    delta_values,
    delta_exponents,
):
    replicas = lax.axis_size("replica")
    devices = lax.axis_size("fsdp")
    chips = devices // 2
    me = lax.axis_index("fsdp")
    chip, core = me // 2, me % 2
    position = chip + core * (chips - 1 - 2 * chip)
    way = 1 - 2 * core
    behind = [(chip - way * s + chips) % chips for s in range(chips)]
    order = Order(jnp.stack([*behind, position, core]).astype(jnp.int32))
    shard = value_weight.shape[1]
    block = 2 * shard
    bf16, f32 = jnp.bfloat16, jnp.float32

    def swap(value):
        return lax.ppermute(value, "fsdp", [(i, i ^ 1) for i in range(devices)])

    def move(value, active=lambda y: True):
        return lax.ppermute(value, "fsdp", move_perm(chips, active))

    class Gradient:
        def __init__(self, mid, x, after=()):
            terms = lax.dot_general(mid, x, (((0,), (0,)), ((), ())), preferred_element_type=f32)
            self.terms = terms.astype(bf16)
            if after:
                self.terms = fence(order, self.terms, after=after)[0]
            self.across = [None] + [swap(self.block(chips - s)) for s in range(1, chips)]
            self.arrived = None

        def block(self, place):
            return self.terms[:, place * block : (place + 1) * block]

        def message(self, step):
            term = self.block(step).astype(f32) + self.across[step].astype(f32)
            if self.arrived is not None:
                term = term + self.arrived.astype(f32)
            return term.astype(bf16)

        def reduce(self, step):
            message = self.message(step)
            self.arrived = move(message, lambda y: y <= step - 1)
            return message

        def finish(self):
            whole = self.block(0).astype(f32) + self.arrived.astype(f32)
            first, second = whole[:, :shard], whole[:, shard:]
            mine = jnp.where(core == 0, first, second)
            partners = jnp.where(core == 0, second, first)
            return (mine + swap(partners.astype(bf16)).astype(f32)).T

    def gather(own, at_first=False):
        along = list(own)
        pieces, others = [list(along)], []
        for step in range(1, chips):
            along = [move(part, lambda y: y >= step - 1) for part in along]
            if at_first and step == 1:
                along[:1] = fence(order, along[0])
            pieces.append(list(along))
            others.append([swap(part) for part in along])
        return pieces, others

    def assemble(pieces, others):
        shards = [jnp.concatenate(pieces[0], axis=1)]
        for p in range(1, chips):
            parts = zip(pieces[p], others[chips - p - 1])
            chosen = [jnp.where(position >= p, here, there) for here, there in parts]
            shards.append(jnp.concatenate(chosen, axis=1))
        return jnp.concatenate(shards, axis=0)

    first_own, second_own = value_weight[0], output_weight[0]
    first_partner, second_partner = swap(first_own), swap(second_own)

    joined = join_cores(order, first_own, first_partner, HALVES, (second_partner,))
    normed, cotangent = prepare(order, tokens[0], out_cotangent[0], norm_gain, chips)
    exponents = fence(order, delta_exponents)[0]
    bits = replicas.bit_length() - 1
    if replicas != 1 << bits or bits < 1:
        raise ValueError("replicas")
    rows_half = base_params.shape[0] // 2
    sums, early = [], []
    for index in range(2):
        rows = slice(index * rows_half, (index + 1) * rows_half)
        scale = jnp.exp2(exponents[0, rows].astype(f32))[:, None]
        total = delta_values[0, rows].astype(f32) * scale
        for turn in range(bits):
            mine = total.astype(bf16)
            bit = 1 << ((turn + index) % bits)
            theirs = lax.ppermute(mine, "replica", [(i, i ^ bit) for i in range(replicas)])
            if turn == 0:
                early.append(theirs)
            total = mine.astype(f32) + theirs.astype(f32)
        sums.append((mine, theirs))
    pieces, others = gather(joined, at_first=True)
    last = pieces[-1]

    joined = join_cores(order, second_own, second_partner, 1, (last[0],))
    weight = assemble(pieces, others)
    weight = fence(order, weight)[0]
    values = jnp.dot(normed, weight, preferred_element_type=f32).astype(bf16)
    pieces, others = gather(joined)
    values = fence(order, values, after=(pieces[1][0], *early))[0]
    first = Gradient(values, cotangent, (pieces[2][0],))
    sent = [first.reduce(step) for step in range(1, chips)]

    weight = assemble(pieces, others)
    weight = fence(order, weight)[0]
    mid = jnp.dot(cotangent, weight, preferred_element_type=f32).astype(bf16)
    mid = fence(order, mid, after=(sent[-1],))[0]
    half = mid.shape[1] // HALVES
    second = []
    for j in range(HALVES):
        after = () if j else ()
        second.append(Gradient(mid[:, j * half : (j + 1) * half], normed, after))
    for step in range(1, chips):
        sent = tuple(gradient.reduce(step) for gradient in second)
        if step == 1:
            theirs = fence(order, *(pair[1] for pair in sums), after=sent)
    output_grad = first.finish()

    total = [a.astype(f32) + b.astype(f32) for (a, _), b in zip(sums, theirs)]
    delta = jnp.concatenate(total) * (1.0 / replicas)
    new_base, new_momentum = nesterov(delta, base_params, outer_momentum)
    value_grad = jnp.concatenate([gradient.finish() for gradient in second], axis=1)
    return (value_grad[None], output_grad[None], new_base, new_momentum)


def solution(mesh):
    return jax.shard_map(
        per_device,
        mesh=mesh,
        in_specs=(
            P("replica", "fsdp", None),
            P(),
            P("replica", "fsdp", None),
            P("replica", "fsdp", None),
            P("replica", "fsdp", None),
            P("fsdp", None),
            P("fsdp", None),
            P("replica", "fsdp", None),
            P("replica", "fsdp"),
        ),
        out_specs=(
            P("replica", "fsdp", None),
            P("replica", "fsdp", None),
            P("fsdp", None),
            P("fsdp", None),
        ),
        check_vma=False,
    )
```

```python
import jax
import jax.numpy as jnp
from jax import lax
from jax.experimental import pallas as pl
from jax.experimental.pallas import tpu as pltpu
from jax.sharding import PartitionSpec as P

HALVES = 2
ROW_TILE = 128
FLOPS_PER_US = 10**9
ANY = pl.BlockSpec(memory_space=pl.ANY)


def move_perm(chips, active):
    pairs = []
    for z in range(chips):
        if z < chips - 1 and active(z):
            pairs.append((2 * z, 2 * z + 2))
        if z > 0 and active(chips - 1 - z):
            pairs.append((2 * z + 1, 2 * z - 1))
    return pairs


class Order:
    def __init__(self, place):
        self.place = place
        self.last = ()

    def __call__(
        self, kernel, args, in_specs, out_shape, scratch, vmem, after=(), aliases=None, grid=1,
        out_specs=None, us=1.0,
    ):
        after = self.last + tuple(after)
        count = len(args)

        def ordered(place_ref, *refs):
            kernel(place_ref, *refs[:count], *refs[count + len(after) :])

        result = pl.pallas_call(
            ordered,
            grid_spec=pltpu.PrefetchScalarGridSpec(
                num_scalar_prefetch=1,
                grid=(grid,),
                in_specs=in_specs + [ANY] * len(after),
                out_specs=out_specs or [ANY] * len(out_shape),
                scratch_shapes=scratch,
            ),
            out_shape=out_shape,
            input_output_aliases={1 + i: o for i, o in (aliases or {}).items()},
            compiler_params=pltpu.CompilerParams(vmem_limit_bytes=vmem * 1024 * 1024),
            cost_estimate=pl.CostEstimate(flops=int(us * FLOPS_PER_US), bytes_accessed=1, transcendentals=0),
            name=kernel.__qualname__.split(".")[0],
        )(self.place, *args, *after)
        self.last = (result[0],)
        return result


def copies(pairs, sems):
    started = [pltpu.make_async_copy(a, b, sems.at[i]) for i, (a, b) in enumerate(pairs)]
    for copy in started:
        copy.start()
    return started


def fence(order, *values, after=()):
    def fence(*refs):
        pass

    shapes = [jax.ShapeDtypeStruct(v.shape, v.dtype) for v in values]
    aliases = {i: i for i in range(len(values))}
    return order(fence, values, [ANY] * len(values), shapes, [], 4, after, aliases)


def prepare(order, tokens, cotangent, gain, chips, after=()):
    rows, model = tokens.shape
    block = model // chips

    def run(place_ref, tokens_ref, cot_ref, gain_ref, normed_out, cot_out):
        xf = tokens_ref[...].astype(jnp.float32)
        scale = lax.rsqrt(jnp.mean(xf * xf, axis=1, keepdims=True) + 1e-05)
        for p in range(chips):
            cols = pl.ds(pl.multiple_of(place_ref[p] * block, block), block)
            to = slice(p * block, (p + 1) * block)
            part = tokens_ref[:, cols].astype(jnp.float32)
            normed_out[:, to] = (part * scale * gain_ref[:, cols]).astype(jnp.bfloat16)
            cot_out[:, to] = cot_ref[:, cols]

    tile = pl.BlockSpec((ROW_TILE, model), lambda i, _: (i, 0))
    return order(
        run,
        (tokens, cotangent, gain[None]),
        [tile, tile, pl.BlockSpec((1, model), lambda i, _: (0, 0))],
        [jax.ShapeDtypeStruct((rows, model), jnp.bfloat16)] * 2,
        [],
        24,
        after,
        grid=rows // ROW_TILE,
        out_specs=[tile, tile],
        us=20.0,
    )


def join_cores(order, own, partner, parts, after=()):
    rows, features = own.shape
    piece = features // parts

    def run(place_ref, own_ref, partner_ref, *refs):
        out_refs, sems = refs[:parts], refs[parts]
        core = place_ref[place_ref.shape[0] - 1]
        pairs = []
        for j, out_ref in enumerate(out_refs):
            cols = pl.ds(j * piece, piece)
            for source, where in ((own_ref, core), (partner_ref, 1 - core)):
                target = out_ref.at[pl.ds(pl.multiple_of(where * rows, rows), rows)]
                pairs.append((source.at[:, cols], target))
        for copy in copies(pairs, sems):
            copy.wait()

    return order(
        run,
        (own, partner),
        [ANY, ANY],
        [jax.ShapeDtypeStruct((2 * rows, piece), jnp.bfloat16)] * parts,
        [pltpu.SemaphoreType.DMA((2 * parts,))],
        4,
        after,
    )


def nesterov(delta, base_part, momentum_part):
    momentum_next = 0.9 * momentum_part + delta
    base_next = (base_part.astype(jnp.float32) - 0.7 * (delta + 0.9 * momentum_next)).astype(
        jnp.bfloat16
    )
    return (base_next, momentum_next)


def per_device(
    tokens,
    norm_gain,
    value_weight,
    output_weight,
    out_cotangent,
    base_params,
    outer_momentum,
    delta_values,
    delta_exponents,
):
    replicas = lax.axis_size("replica")
    devices = lax.axis_size("fsdp")
    chips = devices // 2
    me = lax.axis_index("fsdp")
    chip, core = me // 2, me % 2
    position = chip + core * (chips - 1 - 2 * chip)
    way = 1 - 2 * core
    behind = [(chip - way * s + chips) % chips for s in range(chips)]
    order = Order(jnp.stack([*behind, position, core]).astype(jnp.int32))
    shard = value_weight.shape[1]
    block = 2 * shard
    bf16, f32 = jnp.bfloat16, jnp.float32

    def swap(value):
        return lax.ppermute(value, "fsdp", [(i, i ^ 1) for i in range(devices)])

    def move(value, active=lambda y: True):
        return lax.ppermute(value, "fsdp", move_perm(chips, active))

    class Gradient:
        def __init__(self, mid, x, after=()):
            terms = lax.dot_general(mid, x, (((0,), (0,)), ((), ())), preferred_element_type=f32)
            self.terms = terms.astype(bf16)
            if after:
                self.terms = fence(order, self.terms, after=after)[0]
            self.across = [None] + [swap(self.block(chips - s)) for s in range(1, chips)]
            self.arrived = None

        def block(self, place):
            return self.terms[:, place * block : (place + 1) * block]

        def message(self, step):
            term = self.block(step).astype(f32) + self.across[step].astype(f32)
            if self.arrived is not None:
                term = term + self.arrived.astype(f32)
            return term.astype(bf16)

        def reduce(self, step):
            message = self.message(step)
            self.arrived = move(message, lambda y: y <= step - 1)
            return message

        def finish(self):
            whole = self.block(0).astype(f32) + self.arrived.astype(f32)
            first, second = whole[:, :shard], whole[:, shard:]
            mine = jnp.where(core == 0, first, second)
            partners = jnp.where(core == 0, second, first)
            return (mine + swap(partners.astype(bf16)).astype(f32)).T

    def gather(own, at_first=False):
        along = list(own)
        pieces, others = [list(along)], []
        for step in range(1, chips):
            along = [move(part, lambda y: y >= step - 1) for part in along]
            if at_first and step == 1:
                along[:1] = fence(order, along[0])
            pieces.append(list(along))
            others.append([swap(part) for part in along])
        return pieces, others

    def assemble(pieces, others):
        parts = []
        for j, first in enumerate(pieces[0]):
            shards = [first]
            for p in range(1, chips):
                here, there = pieces[p][j], others[chips - p - 1][j]
                shards.append(jnp.where(position >= p, here, there))
            parts.append(jnp.concatenate(shards, axis=0))
        return fence(order, *parts)

    first_own, second_own = value_weight[0], output_weight[0]
    first_partner, second_partner = swap(first_own), swap(second_own)

    joined = join_cores(order, first_own, first_partner, HALVES, (second_partner,))
    normed, cotangent = prepare(order, tokens[0], out_cotangent[0], norm_gain, chips)
    pieces, others = gather(joined, at_first=True)
    last = pieces[-1]

    exponents = fence(order, delta_exponents, after=(pieces[2][1],))[0]
    bits = replicas.bit_length() - 1
    if replicas != 1 << bits or bits < 1:
        raise ValueError("replicas")
    rows_half = base_params.shape[0] // 2
    sums, early = [], []
    for index in range(2):
        rows = slice(index * rows_half, (index + 1) * rows_half)
        scale = jnp.exp2(exponents[0, rows].astype(f32))[:, None]
        total = delta_values[0, rows].astype(f32) * scale
        for turn in range(bits):
            mine = total.astype(bf16)
            bit = 1 << ((turn + index) % bits)
            theirs = lax.ppermute(mine, "replica", [(i, i ^ bit) for i in range(replicas)])
            if turn == 0:
                early.append(theirs)
            total = mine.astype(f32) + theirs.astype(f32)
        sums.append((mine, theirs))

    joined = join_cores(order, second_own, second_partner, 1, (last[0],))
    values = jnp.concatenate(
        [
            jnp.dot(normed, part, preferred_element_type=f32).astype(bf16)
            for part in assemble(pieces, others)
        ],
        axis=1,
    )
    pieces, others = gather(joined)
    values = fence(order, values, after=(pieces[1][0], *early))[0]
    first = Gradient(values, cotangent, (pieces[2][0],))
    sent = [first.reduce(step) for step in range(1, chips)]

    weight = assemble(pieces, others)[0]
    mid = jnp.dot(cotangent, weight, preferred_element_type=f32).astype(bf16)
    mid = fence(order, mid, after=(sent[-1],))[0]
    half = mid.shape[1] // HALVES
    second = []
    for j in range(HALVES):
        after = () if j else ()
        second.append(Gradient(mid[:, j * half : (j + 1) * half], normed, after))
    for step in range(1, chips):
        sent = tuple(gradient.reduce(step) for gradient in second)
        if step == 1:
            theirs = fence(order, *(pair[1] for pair in sums), after=sent)
    output_grad = first.finish()

    total = [a.astype(f32) + b.astype(f32) for (a, _), b in zip(sums, theirs)]
    delta = jnp.concatenate(total) * (1.0 / replicas)
    new_base, new_momentum = nesterov(delta, base_params, outer_momentum)
    value_grad = jnp.concatenate([gradient.finish() for gradient in second], axis=1)
    return (value_grad[None], output_grad[None], new_base, new_momentum)


def solution(mesh):
    return jax.shard_map(
        per_device,
        mesh=mesh,
        in_specs=(
            P("replica", "fsdp", None),
            P(),
            P("replica", "fsdp", None),
            P("replica", "fsdp", None),
            P("replica", "fsdp", None),
            P("fsdp", None),
            P("fsdp", None),
            P("replica", "fsdp", None),
            P("replica", "fsdp"),
        ),
        out_specs=(
            P("replica", "fsdp", None),
            P("replica", "fsdp", None),
            P("fsdp", None),
            P("fsdp", None),
        ),
        check_vma=False,
    )
```

```python
import jax
import jax.numpy as jnp
from jax import lax
from jax.experimental import pallas as pl
from jax.experimental.pallas import tpu as pltpu
from jax.sharding import PartitionSpec as P

HALVES = 2
ROW_TILE = 128
FLOPS_PER_US = 10**9
ANY = pl.BlockSpec(memory_space=pl.ANY)


def move_perm(chips, active):
    pairs = []
    for z in range(chips):
        if z < chips - 1 and active(z):
            pairs.append((2 * z, 2 * z + 2))
        if z > 0 and active(chips - 1 - z):
            pairs.append((2 * z + 1, 2 * z - 1))
    return pairs


class Order:
    def __init__(self, place):
        self.place = place
        self.last = ()

    def __call__(
        self, kernel, args, in_specs, out_shape, scratch, vmem, after=(), aliases=None, grid=1,
        out_specs=None, us=1.0,
    ):
        after = self.last + tuple(after)
        count = len(args)

        def ordered(place_ref, *refs):
            kernel(place_ref, *refs[:count], *refs[count + len(after) :])

        result = pl.pallas_call(
            ordered,
            grid_spec=pltpu.PrefetchScalarGridSpec(
                num_scalar_prefetch=1,
                grid=(grid,),
                in_specs=in_specs + [ANY] * len(after),
                out_specs=out_specs or [ANY] * len(out_shape),
                scratch_shapes=scratch,
            ),
            out_shape=out_shape,
            input_output_aliases={1 + i: o for i, o in (aliases or {}).items()},
            compiler_params=pltpu.CompilerParams(vmem_limit_bytes=vmem * 1024 * 1024),
            cost_estimate=pl.CostEstimate(flops=int(us * FLOPS_PER_US), bytes_accessed=1, transcendentals=0),
            name=kernel.__qualname__.split(".")[0],
        )(self.place, *args, *after)
        self.last = (result[0],)
        return result


def copies(pairs, sems):
    started = [pltpu.make_async_copy(a, b, sems.at[i]) for i, (a, b) in enumerate(pairs)]
    for copy in started:
        copy.start()
    return started


def fence(order, *values, after=()):
    def fence(*refs):
        pass

    shapes = [jax.ShapeDtypeStruct(v.shape, v.dtype) for v in values]
    aliases = {i: i for i in range(len(values))}
    return order(fence, values, [ANY] * len(values), shapes, [], 4, after, aliases)


def prepare(order, tokens, cotangent, gain, chips, after=()):
    rows, model = tokens.shape
    block = model // chips

    def run(place_ref, tokens_ref, cot_ref, gain_ref, normed_out, cot_out):
        xf = tokens_ref[...].astype(jnp.float32)
        scale = lax.rsqrt(jnp.mean(xf * xf, axis=1, keepdims=True) + 1e-05)
        for p in range(chips):
            cols = pl.ds(pl.multiple_of(place_ref[p] * block, block), block)
            to = slice(p * block, (p + 1) * block)
            part = tokens_ref[:, cols].astype(jnp.float32)
            normed_out[:, to] = (part * scale * gain_ref[:, cols]).astype(jnp.bfloat16)
            cot_out[:, to] = cot_ref[:, cols]

    tile = pl.BlockSpec((ROW_TILE, model), lambda i, _: (i, 0))
    return order(
        run,
        (tokens, cotangent, gain[None]),
        [tile, tile, pl.BlockSpec((1, model), lambda i, _: (0, 0))],
        [jax.ShapeDtypeStruct((rows, model), jnp.bfloat16)] * 2,
        [],
        24,
        after,
        grid=rows // ROW_TILE,
        out_specs=[tile, tile],
        us=20.0,
    )


def join_cores(order, own, partner, parts, after=()):
    rows, features = own.shape
    piece = features // parts

    def run(place_ref, own_ref, partner_ref, *refs):
        out_refs, sems = refs[:parts], refs[parts]
        core = place_ref[place_ref.shape[0] - 1]
        pairs = []
        for j, out_ref in enumerate(out_refs):
            cols = pl.ds(j * piece, piece)
            for source, where in ((own_ref, core), (partner_ref, 1 - core)):
                target = out_ref.at[pl.ds(pl.multiple_of(where * rows, rows), rows)]
                pairs.append((source.at[:, cols], target))
        for copy in copies(pairs, sems):
            copy.wait()

    return order(
        run,
        (own, partner),
        [ANY, ANY],
        [jax.ShapeDtypeStruct((2 * rows, piece), jnp.bfloat16)] * parts,
        [pltpu.SemaphoreType.DMA((2 * parts,))],
        4,
        after,
    )


def nesterov(delta, base_part, momentum_part):
    momentum_next = 0.9 * momentum_part + delta
    base_next = (base_part.astype(jnp.float32) - 0.7 * (delta + 0.9 * momentum_next)).astype(
        jnp.bfloat16
    )
    return (base_next, momentum_next)


def per_device(
    tokens,
    norm_gain,
    value_weight,
    output_weight,
    out_cotangent,
    base_params,
    outer_momentum,
    delta_values,
    delta_exponents,
):
    replicas = lax.axis_size("replica")
    devices = lax.axis_size("fsdp")
    chips = devices // 2
    me = lax.axis_index("fsdp")
    chip, core = me // 2, me % 2
    position = chip + core * (chips - 1 - 2 * chip)
    way = 1 - 2 * core
    behind = [(chip - way * s + chips) % chips for s in range(chips)]
    order = Order(jnp.stack([*behind, position, core]).astype(jnp.int32))
    shard = value_weight.shape[1]
    block = 2 * shard
    bf16, f32 = jnp.bfloat16, jnp.float32

    def swap(value):
        return lax.ppermute(value, "fsdp", [(i, i ^ 1) for i in range(devices)])

    def move(value, active=lambda y: True):
        return lax.ppermute(value, "fsdp", move_perm(chips, active))

    class Gradient:
        def __init__(self, mid, x, after=()):
            terms = lax.dot_general(mid, x, (((0,), (0,)), ((), ())), preferred_element_type=f32)
            self.terms = terms.astype(bf16)
            if after:
                self.terms = fence(order, self.terms, after=after)[0]
            self.across = [None] + [swap(self.block(chips - s)) for s in range(1, chips)]
            self.arrived = None

        def block(self, place):
            return self.terms[:, place * block : (place + 1) * block]

        def message(self, step):
            term = self.block(step).astype(f32) + self.across[step].astype(f32)
            if self.arrived is not None:
                term = term + self.arrived.astype(f32)
            return term.astype(bf16)

        def reduce(self, step):
            message = self.message(step)
            self.arrived = move(message, lambda y: y <= step - 1)
            return message

        def finish(self):
            whole = self.block(0).astype(f32) + self.arrived.astype(f32)
            first, second = whole[:, :shard], whole[:, shard:]
            mine = jnp.where(core == 0, first, second)
            partners = jnp.where(core == 0, second, first)
            return (mine + swap(partners.astype(bf16)).astype(f32)).T

    def gather(own):
        along = list(own)
        pieces, others = [list(along)], []
        for step in range(1, chips):
            along = [move(part, lambda y: y >= step - 1) for part in along]
            pieces.append(list(along))
            others.append([swap(part) for part in along])
        return pieces, others

    def assemble(pieces, others, after=()):
        parts = []
        for j, first in enumerate(pieces[0]):
            shards = [first]
            for p in range(1, chips):
                here, there = pieces[p][j], others[chips - p - 1][j]
                shards.append(jnp.where(position >= p, here, there))
            parts.append(jnp.concatenate(shards, axis=0))
        return fence(order, *parts, after=after)

    first_own, second_own = value_weight[0], output_weight[0]
    first_partner, second_partner = swap(first_own), swap(second_own)

    joined = join_cores(order, first_own, first_partner, HALVES, (second_partner,))
    pieces, others = gather(joined)
    last = pieces[-1]

    exponents = fence(order, delta_exponents, after=(pieces[2][1],))[0]
    bits = replicas.bit_length() - 1
    if replicas != 1 << bits or bits < 1:
        raise ValueError("replicas")
    rows_half = base_params.shape[0] // 2
    sums, early = [], []
    for index in range(2):
        rows = slice(index * rows_half, (index + 1) * rows_half)
        scale = jnp.exp2(exponents[0, rows].astype(f32))[:, None]
        total = delta_values[0, rows].astype(f32) * scale
        for turn in range(bits):
            mine = total.astype(bf16)
            bit = 1 << ((turn + index) % bits)
            theirs = lax.ppermute(mine, "replica", [(i, i ^ bit) for i in range(replicas)])
            if turn == 0:
                early.append(theirs)
            total = mine.astype(f32) + theirs.astype(f32)
        sums.append((mine, theirs))

    joined = join_cores(order, second_own, second_partner, 1, (last[0],))
    ahead = gather(joined)
    normed, cotangent = prepare(order, tokens[0], out_cotangent[0], norm_gain, chips, (*others[-1], *others[-2]))
    values = jnp.concatenate(
        [
            jnp.dot(normed, part, preferred_element_type=f32).astype(bf16)
            for part in assemble(pieces, others, (ahead[0][1][0],))
        ],
        axis=1,
    )
    pieces, others = ahead
    values = fence(order, values, after=(pieces[1][0], *early))[0]
    first = Gradient(values, cotangent, (pieces[2][0],))
    sent = [first.reduce(step) for step in range(1, chips)]

    weight = assemble(pieces, others)[0]
    mid = jnp.dot(cotangent, weight, preferred_element_type=f32).astype(bf16)
    mid = fence(order, mid, after=(sent[-1],))[0]
    half = mid.shape[1] // HALVES
    second = []
    for j in range(HALVES):
        after = () if j else ()
        second.append(Gradient(mid[:, j * half : (j + 1) * half], normed, after))
    for step in range(1, chips):
        sent = tuple(gradient.reduce(step) for gradient in second)
        if step == 1:
            theirs = fence(order, *(pair[1] for pair in sums), after=sent)
    output_grad = first.finish()

    total = [a.astype(f32) + b.astype(f32) for (a, _), b in zip(sums, theirs)]
    delta = jnp.concatenate(total) * (1.0 / replicas)
    new_base, new_momentum = nesterov(delta, base_params, outer_momentum)
    value_grad = jnp.concatenate([gradient.finish() for gradient in second], axis=1)
    return (value_grad[None], output_grad[None], new_base, new_momentum)


def solution(mesh):
    return jax.shard_map(
        per_device,
        mesh=mesh,
        in_specs=(
            P("replica", "fsdp", None),
            P(),
            P("replica", "fsdp", None),
            P("replica", "fsdp", None),
            P("replica", "fsdp", None),
            P("fsdp", None),
            P("fsdp", None),
            P("replica", "fsdp", None),
            P("replica", "fsdp"),
        ),
        out_specs=(
            P("replica", "fsdp", None),
            P("replica", "fsdp", None),
            P("fsdp", None),
            P("fsdp", None),
        ),
        check_vma=False,
    )
```

```python
import jax
import jax.numpy as jnp
from jax import lax
from jax.experimental import pallas as pl
from jax.experimental.pallas import tpu as pltpu
from jax.sharding import PartitionSpec as P

HALVES = 2
ROW_TILE = 128
FLOPS_PER_US = 10**9
ANY = pl.BlockSpec(memory_space=pl.ANY)


def move_perm(chips, active):
    pairs = []
    for z in range(chips):
        if z < chips - 1 and active(z):
            pairs.append((2 * z, 2 * z + 2))
        if z > 0 and active(chips - 1 - z):
            pairs.append((2 * z + 1, 2 * z - 1))
    return pairs


class Order:
    def __init__(self, place):
        self.place = place
        self.last = ()

    def __call__(
        self, kernel, args, in_specs, out_shape, scratch, vmem, after=(), aliases=None, grid=1,
        out_specs=None, us=1.0,
    ):
        after = self.last + tuple(after)
        count = len(args)

        def ordered(place_ref, *refs):
            kernel(place_ref, *refs[:count], *refs[count + len(after) :])

        result = pl.pallas_call(
            ordered,
            grid_spec=pltpu.PrefetchScalarGridSpec(
                num_scalar_prefetch=1,
                grid=(grid,),
                in_specs=in_specs + [ANY] * len(after),
                out_specs=out_specs or [ANY] * len(out_shape),
                scratch_shapes=scratch,
            ),
            out_shape=out_shape,
            input_output_aliases={1 + i: o for i, o in (aliases or {}).items()},
            compiler_params=pltpu.CompilerParams(vmem_limit_bytes=vmem * 1024 * 1024),
            cost_estimate=pl.CostEstimate(flops=int(us * FLOPS_PER_US), bytes_accessed=1, transcendentals=0),
            name=kernel.__qualname__.split(".")[0],
        )(self.place, *args, *after)
        self.last = (result[0],)
        return result


def copies(pairs, sems):
    started = [pltpu.make_async_copy(a, b, sems.at[i]) for i, (a, b) in enumerate(pairs)]
    for copy in started:
        copy.start()
    return started


def fence(order, *values, after=()):
    def fence(*refs):
        pass

    shapes = [jax.ShapeDtypeStruct(v.shape, v.dtype) for v in values]
    aliases = {i: i for i in range(len(values))}
    return order(fence, values, [ANY] * len(values), shapes, [], 4, after, aliases)


def prepare(order, tokens, cotangent, gain, chips, after=()):
    rows, model = tokens.shape
    block = model // chips

    def run(place_ref, tokens_ref, cot_ref, gain_ref, normed_out, cot_out):
        xf = tokens_ref[...].astype(jnp.float32)
        scale = lax.rsqrt(jnp.mean(xf * xf, axis=1, keepdims=True) + 1e-05)
        for p in range(chips):
            cols = pl.ds(pl.multiple_of(place_ref[p] * block, block), block)
            to = slice(p * block, (p + 1) * block)
            part = tokens_ref[:, cols].astype(jnp.float32)
            normed_out[:, to] = (part * scale * gain_ref[:, cols]).astype(jnp.bfloat16)
            cot_out[:, to] = cot_ref[:, cols]

    tile = pl.BlockSpec((ROW_TILE, model), lambda i, _: (i, 0))
    return order(
        run,
        (tokens, cotangent, gain[None]),
        [tile, tile, pl.BlockSpec((1, model), lambda i, _: (0, 0))],
        [jax.ShapeDtypeStruct((rows, model), jnp.bfloat16)] * 2,
        [],
        24,
        after,
        grid=rows // ROW_TILE,
        out_specs=[tile, tile],
        us=20.0,
    )


def join_cores(order, own, partner, parts, after=()):
    rows, features = own.shape
    piece = features // parts

    def run(place_ref, own_ref, partner_ref, *refs):
        out_refs, sems = refs[:parts], refs[parts]
        core = place_ref[place_ref.shape[0] - 1]
        pairs = []
        for j, out_ref in enumerate(out_refs):
            cols = pl.ds(j * piece, piece)
            for source, where in ((own_ref, core), (partner_ref, 1 - core)):
                target = out_ref.at[pl.ds(pl.multiple_of(where * rows, rows), rows)]
                pairs.append((source.at[:, cols], target))
        for copy in copies(pairs, sems):
            copy.wait()

    return order(
        run,
        (own, partner),
        [ANY, ANY],
        [jax.ShapeDtypeStruct((2 * rows, piece), jnp.bfloat16)] * parts,
        [pltpu.SemaphoreType.DMA((2 * parts,))],
        4,
        after,
    )


def nesterov(delta, base_part, momentum_part):
    momentum_next = 0.9 * momentum_part + delta
    base_next = (base_part.astype(jnp.float32) - 0.7 * (delta + 0.9 * momentum_next)).astype(
        jnp.bfloat16
    )
    return (base_next, momentum_next)


def per_device(
    tokens,
    norm_gain,
    value_weight,
    output_weight,
    out_cotangent,
    base_params,
    outer_momentum,
    delta_values,
    delta_exponents,
):
    replicas = lax.axis_size("replica")
    devices = lax.axis_size("fsdp")
    chips = devices // 2
    me = lax.axis_index("fsdp")
    chip, core = me // 2, me % 2
    position = chip + core * (chips - 1 - 2 * chip)
    way = 1 - 2 * core
    behind = [(chip - way * s + chips) % chips for s in range(chips)]
    order = Order(jnp.stack([*behind, position, core]).astype(jnp.int32))
    shard = value_weight.shape[1]
    block = 2 * shard
    bf16, f32 = jnp.bfloat16, jnp.float32

    def swap(value):
        return lax.ppermute(value, "fsdp", [(i, i ^ 1) for i in range(devices)])

    def move(value, active=lambda y: True):
        return lax.ppermute(value, "fsdp", move_perm(chips, active))

    class Gradient:
        def __init__(self, mid, x, after=()):
            terms = lax.dot_general(mid, x, (((0,), (0,)), ((), ())), preferred_element_type=f32)
            self.terms = terms.astype(bf16)
            if after:
                self.terms = fence(order, self.terms, after=after)[0]
            self.across = [None] + [swap(self.block(chips - s)) for s in range(1, chips)]
            self.arrived = None

        def block(self, place):
            return self.terms[:, place * block : (place + 1) * block]

        def message(self, step):
            term = self.block(step).astype(f32) + self.across[step].astype(f32)
            if self.arrived is not None:
                term = term + self.arrived.astype(f32)
            return term.astype(bf16)

        def reduce(self, step):
            message = self.message(step)
            self.arrived = move(message, lambda y: y <= step - 1)
            return message

        def finish(self):
            whole = self.block(0).astype(f32) + self.arrived.astype(f32)
            first, second = whole[:, :shard], whole[:, shard:]
            mine = jnp.where(core == 0, first, second)
            partners = jnp.where(core == 0, second, first)
            return (mine + swap(partners.astype(bf16)).astype(f32)).T

    def gather(own):
        along = list(own)
        pieces, others = [list(along)], []
        for step in range(1, chips):
            along = [move(part, lambda y: y >= step - 1) for part in along]
            pieces.append(list(along))
            others.append([swap(part) for part in along])
        return pieces, others

    def assemble(pieces, others, after=()):
        parts = []
        for j, first in enumerate(pieces[0]):
            shards = [first]
            for p in range(1, chips):
                here, there = pieces[p][j], others[chips - p - 1][j]
                shards.append(jnp.where(position >= p, here, there))
            parts.append(jnp.concatenate(shards, axis=0))
        return fence(order, *parts, after=after)

    first_own, second_own = value_weight[0], output_weight[0]
    first_partner, second_partner = swap(first_own), swap(second_own)

    joined = join_cores(order, first_own, first_partner, HALVES, (second_partner,))
    pieces, others = gather(joined)
    last = pieces[-1]

    exponents = fence(order, delta_exponents, after=(pieces[2][1],))[0]
    bits = replicas.bit_length() - 1
    if replicas != 1 << bits or bits < 1:
        raise ValueError("replicas")
    rows_half = base_params.shape[0] // 2
    sums, early = [], []
    for index in range(2):
        rows = slice(index * rows_half, (index + 1) * rows_half)
        scale = jnp.exp2(exponents[0, rows].astype(f32))[:, None]
        total = delta_values[0, rows].astype(f32) * scale
        for turn in range(bits):
            mine = total.astype(bf16)
            bit = 1 << ((turn + index) % bits)
            theirs = lax.ppermute(mine, "replica", [(i, i ^ bit) for i in range(replicas)])
            if turn == 0:
                early.append(theirs)
            total = mine.astype(f32) + theirs.astype(f32)
        sums.append((mine, theirs))

    joined = join_cores(order, second_own, second_partner, 1, (last[0],))
    ahead = gather(joined)
    normed, cotangent = prepare(order, tokens[0], out_cotangent[0], norm_gain, chips, (*others[-1], *others[-2]))
    values = jnp.concatenate(
        [
            jnp.dot(normed, part, preferred_element_type=f32).astype(bf16)
            for part in assemble(pieces, others, (ahead[0][1][0],))
        ],
        axis=1,
    )
    pieces, others = ahead
    values = fence(order, values, after=(pieces[1][0], *early))[0]
    first = Gradient(values, cotangent, (pieces[2][0],))
    sent = [first.reduce(step) for step in range(1, chips)]

    weight = assemble(pieces, others)[0]
    mid = jnp.dot(cotangent, weight, preferred_element_type=f32).astype(bf16)
    mid = fence(order, mid, after=(sent[-1],))[0]
    half = mid.shape[1] // HALVES
    second = []
    for j in range(HALVES):
        after = (first.arrived,) if j else ()
        second.append(Gradient(mid[:, j * half : (j + 1) * half], normed, after))
    for step in range(1, chips):
        sent = tuple(gradient.reduce(step) for gradient in second)
        if step == 1:
            theirs = fence(order, *(pair[1] for pair in sums), after=sent)
    output_grad = first.finish()

    total = [a.astype(f32) + b.astype(f32) for (a, _), b in zip(sums, theirs)]
    delta = jnp.concatenate(total) * (1.0 / replicas)
    new_base, new_momentum = nesterov(delta, base_params, outer_momentum)
    value_grad = jnp.concatenate([gradient.finish() for gradient in second], axis=1)
    return (value_grad[None], output_grad[None], new_base, new_momentum)


def solution(mesh):
    return jax.shard_map(
        per_device,
        mesh=mesh,
        in_specs=(
            P("replica", "fsdp", None),
            P(),
            P("replica", "fsdp", None),
            P("replica", "fsdp", None),
            P("replica", "fsdp", None),
            P("fsdp", None),
            P("fsdp", None),
            P("replica", "fsdp", None),
            P("replica", "fsdp"),
        ),
        out_specs=(
            P("replica", "fsdp", None),
            P("replica", "fsdp", None),
            P("fsdp", None),
            P("fsdp", None),
        ),
        check_vma=False,
    )
```

```python
import jax
import jax.numpy as jnp
from jax import lax
from jax.experimental import pallas as pl
from jax.experimental.pallas import tpu as pltpu
from jax.sharding import PartitionSpec as P

HALVES = 2
ROW_TILE = 128
FLOPS_PER_US = 10**9
ANY = pl.BlockSpec(memory_space=pl.ANY)


def move_perm(chips, active):
    pairs = []
    for z in range(chips):
        if z < chips - 1 and active(z):
            pairs.append((2 * z, 2 * z + 2))
        if z > 0 and active(chips - 1 - z):
            pairs.append((2 * z + 1, 2 * z - 1))
    return pairs


class Order:
    def __init__(self, place):
        self.place = place
        self.last = ()

    def __call__(
        self, kernel, args, in_specs, out_shape, scratch, vmem, after=(), aliases=None, grid=1,
        out_specs=None, us=1.0,
    ):
        after = self.last + tuple(after)
        count = len(args)

        def ordered(place_ref, *refs):
            kernel(place_ref, *refs[:count], *refs[count + len(after) :])

        result = pl.pallas_call(
            ordered,
            grid_spec=pltpu.PrefetchScalarGridSpec(
                num_scalar_prefetch=1,
                grid=(grid,),
                in_specs=in_specs + [ANY] * len(after),
                out_specs=out_specs or [ANY] * len(out_shape),
                scratch_shapes=scratch,
            ),
            out_shape=out_shape,
            input_output_aliases={1 + i: o for i, o in (aliases or {}).items()},
            compiler_params=pltpu.CompilerParams(vmem_limit_bytes=vmem * 1024 * 1024),
            cost_estimate=pl.CostEstimate(flops=int(us * FLOPS_PER_US), bytes_accessed=1, transcendentals=0),
            name=kernel.__qualname__.split(".")[0],
        )(self.place, *args, *after)
        self.last = (result[0],)
        return result


def copies(pairs, sems):
    started = [pltpu.make_async_copy(a, b, sems.at[i]) for i, (a, b) in enumerate(pairs)]
    for copy in started:
        copy.start()
    return started


def fence(order, *values, after=()):
    def fence(*refs):
        pass

    shapes = [jax.ShapeDtypeStruct(v.shape, v.dtype) for v in values]
    aliases = {i: i for i in range(len(values))}
    return order(fence, values, [ANY] * len(values), shapes, [], 4, after, aliases)


def in_places(order, x, gain, chips, after=()):
    rows, model = x.shape
    block = model // chips

    def run(place_ref, x_ref, *refs):
        out_ref = refs[-1]
        if gain is not None:
            xf = x_ref[...].astype(jnp.float32)
            scale = lax.rsqrt(jnp.mean(xf * xf, axis=1, keepdims=True) + 1e-05)
        for p in range(chips):
            cols = pl.ds(pl.multiple_of(place_ref[p] * block, block), block)
            part = x_ref[:, cols]
            if gain is not None:
                part = part.astype(jnp.float32) * scale * refs[0][:, cols]
            out_ref[:, p * block : (p + 1) * block] = part.astype(jnp.bfloat16)

    tile = pl.BlockSpec((ROW_TILE, model), lambda i, _: (i, 0))
    gains = () if gain is None else (gain[None],)
    return order(
        run,
        (x, *gains),
        [tile] + [pl.BlockSpec((1, model), lambda i, _: (0, 0))] * len(gains),
        [jax.ShapeDtypeStruct((rows, model), jnp.bfloat16)],
        [],
        16,
        after,
        grid=rows // ROW_TILE,
        out_specs=[tile],
        us=5.0,
    )[0]


def join_cores(order, own, partner, parts, after=()):
    rows, features = own.shape
    piece = features // parts

    def run(place_ref, own_ref, partner_ref, *refs):
        out_refs, sems = refs[:parts], refs[parts]
        core = place_ref[place_ref.shape[0] - 1]
        pairs = []
        for j, out_ref in enumerate(out_refs):
            cols = pl.ds(j * piece, piece)
            for source, where in ((own_ref, core), (partner_ref, 1 - core)):
                target = out_ref.at[pl.ds(pl.multiple_of(where * rows, rows), rows)]
                pairs.append((source.at[:, cols], target))
        for copy in copies(pairs, sems):
            copy.wait()

    return order(
        run,
        (own, partner),
        [ANY, ANY],
        [jax.ShapeDtypeStruct((2 * rows, piece), jnp.bfloat16)] * parts,
        [pltpu.SemaphoreType.DMA((2 * parts,))],
        4,
        after,
    )


def nesterov(delta, base_part, momentum_part):
    momentum_next = 0.9 * momentum_part + delta
    base_next = (base_part.astype(jnp.float32) - 0.7 * (delta + 0.9 * momentum_next)).astype(
        jnp.bfloat16
    )
    return (base_next, momentum_next)


def per_device(
    tokens,
    norm_gain,
    value_weight,
    output_weight,
    out_cotangent,
    base_params,
    outer_momentum,
    delta_values,
    delta_exponents,
):
    replicas = lax.axis_size("replica")
    devices = lax.axis_size("fsdp")
    chips = devices // 2
    me = lax.axis_index("fsdp")
    chip, core = me // 2, me % 2
    position = chip + core * (chips - 1 - 2 * chip)
    way = 1 - 2 * core
    behind = [(chip - way * s + chips) % chips for s in range(chips)]
    order = Order(jnp.stack([*behind, position, core]).astype(jnp.int32))
    shard = value_weight.shape[1]
    block = 2 * shard
    bf16, f32 = jnp.bfloat16, jnp.float32

    def swap(value):
        return lax.ppermute(value, "fsdp", [(i, i ^ 1) for i in range(devices)])

    def move(value, active=lambda y: True):
        return lax.ppermute(value, "fsdp", move_perm(chips, active))

    class Gradient:
        def __init__(self, mid, x, after=(), late=()):
            terms = lax.dot_general(mid, x, (((0,), (0,)), ((), ())), preferred_element_type=f32)
            self.terms = terms.astype(bf16)
            if after:
                self.terms = fence(order, self.terms, after=after)[0]
            self.across = [None] + [swap(self.block(chips - s)) for s in range(1, chips)]
            self.arrived = None
            if late:
                self.across[1] = fence(order, self.across[1], after=late)[0]

        def block(self, place):
            return self.terms[:, place * block : (place + 1) * block]

        def message(self, step):
            term = self.block(step).astype(f32) + self.across[step].astype(f32)
            if self.arrived is not None:
                term = term + self.arrived.astype(f32)
            return term.astype(bf16)

        def reduce(self, step):
            message = self.message(step)
            self.arrived = move(message, lambda y: y <= step - 1)
            return message

        def finish(self):
            whole = self.block(0).astype(f32) + self.arrived.astype(f32)
            first, second = whole[:, :shard], whole[:, shard:]
            mine = jnp.where(core == 0, first, second)
            partners = jnp.where(core == 0, second, first)
            return (mine + swap(partners.astype(bf16)).astype(f32)).T

    def gather(own):
        along = list(own)
        pieces, others = [list(along)], []
        for step in range(1, chips):
            along = [move(part, lambda y: y >= step - 1) for part in along]
            pieces.append(list(along))
            others.append([swap(part) for part in along])
        return pieces, others

    def assemble(pieces, others, after=()):
        parts = []
        for j, first in enumerate(pieces[0]):
            shards = [first]
            for p in range(1, chips):
                here, there = pieces[p][j], others[chips - p - 1][j]
                shards.append(jnp.where(position >= p, here, there))
            parts.append(jnp.concatenate(shards, axis=0))
        return fence(order, *parts, after=after)

    first_own, second_own = value_weight[0], output_weight[0]
    first_partner, second_partner = swap(first_own), swap(second_own)

    joined = join_cores(order, first_own, first_partner, HALVES, (second_partner,))
    pieces, others = gather(joined)
    last = pieces[-1]

    exponents = fence(order, delta_exponents, after=(pieces[2][1],))[0]
    bits = replicas.bit_length() - 1
    if replicas != 1 << bits or bits < 1:
        raise ValueError("replicas")
    rows_half = base_params.shape[0] // 2
    sums, early = [], []
    for index in range(2):
        rows = slice(index * rows_half, (index + 1) * rows_half)
        scale = jnp.exp2(exponents[0, rows].astype(f32))[:, None]
        total = delta_values[0, rows].astype(f32) * scale
        for turn in range(bits):
            mine = total.astype(bf16)
            bit = 1 << ((turn + index) % bits)
            theirs = lax.ppermute(mine, "replica", [(i, i ^ bit) for i in range(replicas)])
            if turn == 0:
                early.append(theirs)
            total = mine.astype(f32) + theirs.astype(f32)
        sums.append((mine, theirs))

    joined = join_cores(order, second_own, second_partner, 1, (last[0],))
    ahead = gather(joined)
    normed = in_places(order, tokens[0], norm_gain, chips, (*others[-1], *others[-2]))
    values = jnp.concatenate(
        [
            jnp.dot(normed, part, preferred_element_type=f32).astype(bf16)
            for part in assemble(pieces, others, (ahead[0][1][0],))
        ],
        axis=1,
    )
    cotangent = in_places(order, out_cotangent[0], None, chips)
    pieces, others = ahead
    values = fence(order, values, after=(pieces[1][0], *early))[0]
    first = Gradient(values, cotangent, (pieces[2][0],))
    sent = [first.reduce(step) for step in range(1, chips)]

    weight = assemble(pieces, others)[0]
    mid = jnp.dot(cotangent, weight, preferred_element_type=f32).astype(bf16)
    mid = fence(order, mid, after=(sent[-1],))[0]
    half = mid.shape[1] // HALVES
    second = []
    for j in range(HALVES):
        late = () if j else ()
        second.append(Gradient(mid[:, j * half : (j + 1) * half], normed, (), late))
    for step in range(1, chips):
        sent = tuple(gradient.reduce(step) for gradient in second)
        if step == 1:
            theirs = fence(order, *(pair[1] for pair in sums), after=sent)
    output_grad = first.finish()

    total = [a.astype(f32) + b.astype(f32) for (a, _), b in zip(sums, theirs)]
    delta = jnp.concatenate(total) * (1.0 / replicas)
    new_base, new_momentum = nesterov(delta, base_params, outer_momentum)
    value_grad = jnp.concatenate([gradient.finish() for gradient in second], axis=1)
    return (value_grad[None], output_grad[None], new_base, new_momentum)


def solution(mesh):
    return jax.shard_map(
        per_device,
        mesh=mesh,
        in_specs=(
            P("replica", "fsdp", None),
            P(),
            P("replica", "fsdp", None),
            P("replica", "fsdp", None),
            P("replica", "fsdp", None),
            P("fsdp", None),
            P("fsdp", None),
            P("replica", "fsdp", None),
            P("replica", "fsdp"),
        ),
        out_specs=(
            P("replica", "fsdp", None),
            P("replica", "fsdp", None),
            P("fsdp", None),
            P("fsdp", None),
        ),
        check_vma=False,
    )
```

```python
import jax
import jax.numpy as jnp
from jax import lax
from jax.experimental import pallas as pl
from jax.experimental.pallas import tpu as pltpu
from jax.sharding import PartitionSpec as P

HALVES = 2
ROW_TILE = 128
FLOPS_PER_US = 10**9
ANY = pl.BlockSpec(memory_space=pl.ANY)


def move_perm(chips, active):
    pairs = []
    for z in range(chips):
        if z < chips - 1 and active(z):
            pairs.append((2 * z, 2 * z + 2))
        if z > 0 and active(chips - 1 - z):
            pairs.append((2 * z + 1, 2 * z - 1))
    return pairs


class Order:
    def __init__(self, place):
        self.place = place
        self.last = ()

    def __call__(
        self, kernel, args, in_specs, out_shape, scratch, vmem, after=(), aliases=None, grid=1,
        out_specs=None, us=1.0,
    ):
        after = self.last + tuple(after)
        count = len(args)

        def ordered(place_ref, *refs):
            kernel(place_ref, *refs[:count], *refs[count + len(after) :])

        result = pl.pallas_call(
            ordered,
            grid_spec=pltpu.PrefetchScalarGridSpec(
                num_scalar_prefetch=1,
                grid=(grid,),
                in_specs=in_specs + [ANY] * len(after),
                out_specs=out_specs or [ANY] * len(out_shape),
                scratch_shapes=scratch,
            ),
            out_shape=out_shape,
            input_output_aliases={1 + i: o for i, o in (aliases or {}).items()},
            compiler_params=pltpu.CompilerParams(vmem_limit_bytes=vmem * 1024 * 1024),
            cost_estimate=pl.CostEstimate(flops=int(us * FLOPS_PER_US), bytes_accessed=1, transcendentals=0),
            name=kernel.__qualname__.split(".")[0],
        )(self.place, *args, *after)
        self.last = (result[0],)
        return result


def copies(pairs, sems):
    started = [pltpu.make_async_copy(a, b, sems.at[i]) for i, (a, b) in enumerate(pairs)]
    for copy in started:
        copy.start()
    return started


def fence(order, *values, after=()):
    def fence(*refs):
        pass

    shapes = [jax.ShapeDtypeStruct(v.shape, v.dtype) for v in values]
    aliases = {i: i for i in range(len(values))}
    return order(fence, values, [ANY] * len(values), shapes, [], 4, after, aliases)


def in_places(order, x, gain, chips, after=()):
    rows, model = x.shape
    block = model // chips

    def run(place_ref, x_ref, *refs):
        out_ref = refs[-1]
        if gain is not None:
            xf = x_ref[...].astype(jnp.float32)
            scale = lax.rsqrt(jnp.mean(xf * xf, axis=1, keepdims=True) + 1e-05)
        for p in range(chips):
            cols = pl.ds(pl.multiple_of(place_ref[p] * block, block), block)
            part = x_ref[:, cols]
            if gain is not None:
                part = part.astype(jnp.float32) * scale * refs[0][:, cols]
            out_ref[:, p * block : (p + 1) * block] = part.astype(jnp.bfloat16)

    tile = pl.BlockSpec((ROW_TILE, model), lambda i, _: (i, 0))
    gains = () if gain is None else (gain[None],)
    return order(
        run,
        (x, *gains),
        [tile] + [pl.BlockSpec((1, model), lambda i, _: (0, 0))] * len(gains),
        [jax.ShapeDtypeStruct((rows, model), jnp.bfloat16)],
        [],
        16,
        after,
        grid=rows // ROW_TILE,
        out_specs=[tile],
        us=5.0,
    )[0]


def join_cores(order, own, partner, parts, after=()):
    rows, features = own.shape
    piece = features // parts

    def run(place_ref, own_ref, partner_ref, *refs):
        out_refs, sems = refs[:parts], refs[parts]
        core = place_ref[place_ref.shape[0] - 1]
        pairs = []
        for j, out_ref in enumerate(out_refs):
            cols = pl.ds(j * piece, piece)
            for source, where in ((own_ref, core), (partner_ref, 1 - core)):
                target = out_ref.at[pl.ds(pl.multiple_of(where * rows, rows), rows)]
                pairs.append((source.at[:, cols], target))
        for copy in copies(pairs, sems):
            copy.wait()

    return order(
        run,
        (own, partner),
        [ANY, ANY],
        [jax.ShapeDtypeStruct((2 * rows, piece), jnp.bfloat16)] * parts,
        [pltpu.SemaphoreType.DMA((2 * parts,))],
        4,
        after,
    )


def nesterov(delta, base_part, momentum_part):
    momentum_next = 0.9 * momentum_part + delta
    base_next = (base_part.astype(jnp.float32) - 0.7 * (delta + 0.9 * momentum_next)).astype(
        jnp.bfloat16
    )
    return (base_next, momentum_next)


def per_device(
    tokens,
    norm_gain,
    value_weight,
    output_weight,
    out_cotangent,
    base_params,
    outer_momentum,
    delta_values,
    delta_exponents,
):
    replicas = lax.axis_size("replica")
    devices = lax.axis_size("fsdp")
    chips = devices // 2
    me = lax.axis_index("fsdp")
    chip, core = me // 2, me % 2
    position = chip + core * (chips - 1 - 2 * chip)
    way = 1 - 2 * core
    behind = [(chip - way * s + chips) % chips for s in range(chips)]
    order = Order(jnp.stack([*behind, position, core]).astype(jnp.int32))
    shard = value_weight.shape[1]
    block = 2 * shard
    bf16, f32 = jnp.bfloat16, jnp.float32

    def swap(value):
        return lax.ppermute(value, "fsdp", [(i, i ^ 1) for i in range(devices)])

    def move(value, active=lambda y: True):
        return lax.ppermute(value, "fsdp", move_perm(chips, active))

    class Gradient:
        def __init__(self, mid, x, after=(), late=()):
            terms = lax.dot_general(mid, x, (((0,), (0,)), ((), ())), preferred_element_type=f32)
            self.terms = terms.astype(bf16)
            if after:
                self.terms = fence(order, self.terms, after=after)[0]
            self.across = [None] + [swap(self.block(chips - s)) for s in range(1, chips)]
            self.arrived = None
            if late:
                self.across[1] = fence(order, self.across[1], after=late)[0]

        def block(self, place):
            return self.terms[:, place * block : (place + 1) * block]

        def message(self, step):
            term = self.block(step).astype(f32) + self.across[step].astype(f32)
            if self.arrived is not None:
                term = term + self.arrived.astype(f32)
            return term.astype(bf16)

        def reduce(self, step):
            message = self.message(step)
            self.arrived = move(message, lambda y: y <= step - 1)
            return message

        def finish(self):
            whole = self.block(0).astype(f32) + self.arrived.astype(f32)
            first, second = whole[:, :shard], whole[:, shard:]
            mine = jnp.where(core == 0, first, second)
            partners = jnp.where(core == 0, second, first)
            return (mine + swap(partners.astype(bf16)).astype(f32)).T

    def gather(own):
        along = list(own)
        pieces, others = [list(along)], []
        for step in range(1, chips):
            along = [move(part, lambda y: y >= step - 1) for part in along]
            pieces.append(list(along))
            others.append([swap(part) for part in along])
        return pieces, others

    def assemble(pieces, others, after=()):
        parts = []
        for j, first in enumerate(pieces[0]):
            shards = [first]
            for p in range(1, chips):
                here, there = pieces[p][j], others[chips - p - 1][j]
                shards.append(jnp.where(position >= p, here, there))
            parts.append(jnp.concatenate(shards, axis=0))
        return fence(order, *parts, after=after)

    first_own, second_own = value_weight[0], output_weight[0]
    first_partner, second_partner = swap(first_own), swap(second_own)

    joined = join_cores(order, first_own, first_partner, HALVES, (second_partner,))
    pieces, others = gather(joined)
    last = pieces[-1]

    exponents = fence(order, delta_exponents, after=(pieces[2][1],))[0]
    bits = replicas.bit_length() - 1
    if replicas != 1 << bits or bits < 1:
        raise ValueError("replicas")
    rows_half = base_params.shape[0] // 2
    sums, early = [], []
    for index in range(2):
        rows = slice(index * rows_half, (index + 1) * rows_half)
        scale = jnp.exp2(exponents[0, rows].astype(f32))[:, None]
        total = delta_values[0, rows].astype(f32) * scale
        for turn in range(bits):
            mine = total.astype(bf16)
            bit = 1 << ((turn + index) % bits)
            theirs = lax.ppermute(mine, "replica", [(i, i ^ bit) for i in range(replicas)])
            if turn == 0:
                early.append(theirs)
            total = mine.astype(f32) + theirs.astype(f32)
        sums.append((mine, theirs))

    joined = join_cores(order, second_own, second_partner, 1, (last[0],))
    ahead = gather(joined)
    normed = in_places(order, tokens[0], norm_gain, chips, (*others[-1],*others[-2]))
    values = jnp.concatenate(
        [
            jnp.dot(normed, part, preferred_element_type=f32).astype(bf16)
            for part in assemble(pieces, others, (ahead[0][1][0],))
        ],
        axis=1,
    )
    cotangent = in_places(order, out_cotangent[0], None, chips)
    pieces, others = ahead
    values = fence(order, values, after=(pieces[1][0], *early))[0]
    first = Gradient(values, cotangent, (pieces[2][0],))
    sent = [first.reduce(step) for step in range(1, chips)]

    weight = assemble(pieces, others, (sent[1],))[0]
    mid = jnp.dot(cotangent, weight, preferred_element_type=f32).astype(bf16)
    mid = fence(order, mid, after=())[0]
    half = mid.shape[1] // HALVES
    second = []
    for j in range(HALVES):
        late = (sent[-1],) if j else ()
        second.append(Gradient(mid[:, j * half : (j + 1) * half], normed, (), late))
    for step in range(1, chips):
        sent = tuple(gradient.reduce(step) for gradient in second)
        if step == 1:
            theirs = fence(order, *(pair[1] for pair in sums), after=sent)
    output_grad = first.finish()

    total = [a.astype(f32) + b.astype(f32) for (a, _), b in zip(sums, theirs)]
    delta = jnp.concatenate(total) * (1.0 / replicas)
    new_base, new_momentum = nesterov(delta, base_params, outer_momentum)
    value_grad = jnp.concatenate([gradient.finish() for gradient in second], axis=1)
    return (value_grad[None], output_grad[None], new_base, new_momentum)


def solution(mesh):
    return jax.shard_map(
        per_device,
        mesh=mesh,
        in_specs=(
            P("replica", "fsdp", None),
            P(),
            P("replica", "fsdp", None),
            P("replica", "fsdp", None),
            P("replica", "fsdp", None),
            P("fsdp", None),
            P("fsdp", None),
            P("replica", "fsdp", None),
            P("replica", "fsdp"),
        ),
        out_specs=(
            P("replica", "fsdp", None),
            P("replica", "fsdp", None),
            P("fsdp", None),
            P("fsdp", None),
        ),
        check_vma=False,
    )
```

```python
import jax
import jax.numpy as jnp
from jax import lax
from jax.experimental import pallas as pl
from jax.experimental.pallas import tpu as pltpu
from jax.sharding import PartitionSpec as P

HALVES = 2
ROW_TILE = 128
FLOPS_PER_US = 10**9
ANY = pl.BlockSpec(memory_space=pl.ANY)


def move_perm(chips, active):
    pairs = []
    for z in range(chips):
        if z < chips - 1 and active(z):
            pairs.append((2 * z, 2 * z + 2))
        if z > 0 and active(chips - 1 - z):
            pairs.append((2 * z + 1, 2 * z - 1))
    return pairs


class Order:
    def __init__(self, place):
        self.place = place
        self.last = ()

    def __call__(
        self, kernel, args, in_specs, out_shape, scratch, vmem, after=(), aliases=None, grid=1,
        out_specs=None, us=1.0,
    ):
        after = self.last + tuple(after)
        count = len(args)

        def ordered(place_ref, *refs):
            kernel(place_ref, *refs[:count], *refs[count + len(after) :])

        result = pl.pallas_call(
            ordered,
            grid_spec=pltpu.PrefetchScalarGridSpec(
                num_scalar_prefetch=1,
                grid=(grid,),
                in_specs=in_specs + [ANY] * len(after),
                out_specs=out_specs or [ANY] * len(out_shape),
                scratch_shapes=scratch,
            ),
            out_shape=out_shape,
            input_output_aliases={1 + i: o for i, o in (aliases or {}).items()},
            compiler_params=pltpu.CompilerParams(vmem_limit_bytes=vmem * 1024 * 1024),
            cost_estimate=pl.CostEstimate(flops=int(us * FLOPS_PER_US), bytes_accessed=1, transcendentals=0),
            name=kernel.__qualname__.split(".")[0],
        )(self.place, *args, *after)
        self.last = (result[0],)
        return result


def copies(pairs, sems):
    started = [pltpu.make_async_copy(a, b, sems.at[i]) for i, (a, b) in enumerate(pairs)]
    for copy in started:
        copy.start()
    return started


def fence(order, *values, after=()):
    def fence(*refs):
        pass

    shapes = [jax.ShapeDtypeStruct(v.shape, v.dtype) for v in values]
    aliases = {i: i for i in range(len(values))}
    return order(fence, values, [ANY] * len(values), shapes, [], 4, after, aliases)


def in_places(order, x, gain, chips, after=()):
    rows, model = x.shape
    block = model // chips

    def run(place_ref, x_ref, *refs):
        out_ref = refs[-1]
        if gain is not None:
            xf = x_ref[...].astype(jnp.float32)
            scale = lax.rsqrt(jnp.mean(xf * xf, axis=1, keepdims=True) + 1e-05)
        for p in range(chips):
            cols = pl.ds(pl.multiple_of(place_ref[p] * block, block), block)
            part = x_ref[:, cols]
            if gain is not None:
                part = part.astype(jnp.float32) * scale * refs[0][:, cols]
            out_ref[:, p * block : (p + 1) * block] = part.astype(jnp.bfloat16)

    tile = pl.BlockSpec((ROW_TILE, model), lambda i, _: (i, 0))
    gains = () if gain is None else (gain[None],)
    return order(
        run,
        (x, *gains),
        [tile] + [pl.BlockSpec((1, model), lambda i, _: (0, 0))] * len(gains),
        [jax.ShapeDtypeStruct((rows, model), jnp.bfloat16)],
        [],
        16,
        after,
        grid=rows // ROW_TILE,
        out_specs=[tile],
        us=5.0,
    )[0]


def join_cores(order, own, partner, parts, after=()):
    rows, features = own.shape
    piece = features // parts

    def run(place_ref, own_ref, partner_ref, *refs):
        out_refs, sems = refs[:parts], refs[parts]
        core = place_ref[place_ref.shape[0] - 1]
        pairs = []
        for j, out_ref in enumerate(out_refs):
            cols = pl.ds(j * piece, piece)
            for source, where in ((own_ref, core), (partner_ref, 1 - core)):
                target = out_ref.at[pl.ds(pl.multiple_of(where * rows, rows), rows)]
                pairs.append((source.at[:, cols], target))
        for copy in copies(pairs, sems):
            copy.wait()

    return order(
        run,
        (own, partner),
        [ANY, ANY],
        [jax.ShapeDtypeStruct((2 * rows, piece), jnp.bfloat16)] * parts,
        [pltpu.SemaphoreType.DMA((2 * parts,))],
        4,
        after,
    )


def nesterov(delta, base_part, momentum_part):
    momentum_next = 0.9 * momentum_part + delta
    base_next = (base_part.astype(jnp.float32) - 0.7 * (delta + 0.9 * momentum_next)).astype(
        jnp.bfloat16
    )
    return (base_next, momentum_next)


def per_device(
    tokens,
    norm_gain,
    value_weight,
    output_weight,
    out_cotangent,
    base_params,
    outer_momentum,
    delta_values,
    delta_exponents,
):
    replicas = lax.axis_size("replica")
    devices = lax.axis_size("fsdp")
    chips = devices // 2
    me = lax.axis_index("fsdp")
    chip, core = me // 2, me % 2
    position = chip + core * (chips - 1 - 2 * chip)
    way = 1 - 2 * core
    behind = [(chip - way * s + chips) % chips for s in range(chips)]
    order = Order(jnp.stack([*behind, position, core]).astype(jnp.int32))
    shard = value_weight.shape[1]
    block = 2 * shard
    bf16, f32 = jnp.bfloat16, jnp.float32

    def swap(value):
        return lax.ppermute(value, "fsdp", [(i, i ^ 1) for i in range(devices)])

    def move(value, active=lambda y: True):
        return lax.ppermute(value, "fsdp", move_perm(chips, active))

    class Gradient:
        def __init__(self, mid, x, after=()):
            terms = lax.dot_general(mid, x, (((0,), (0,)), ((), ())), preferred_element_type=f32)
            self.terms = terms.astype(bf16)
            if after:
                self.terms = fence(order, self.terms, after=after)[0]
            self.across = [None] + [swap(self.block(chips - s)) for s in range(1, chips)]
            self.arrived = None

        def block(self, place):
            return self.terms[:, place * block : (place + 1) * block]

        def message(self, step):
            term = self.block(step).astype(f32) + self.across[step].astype(f32)
            if self.arrived is not None:
                term = term + self.arrived.astype(f32)
            return term.astype(bf16)

        def reduce(self, step):
            message = self.message(step)
            self.arrived = move(message, lambda y: y <= step - 1)
            return message

        def finish(self):
            whole = self.block(0).astype(f32) + self.arrived.astype(f32)
            first, second = whole[:, :shard], whole[:, shard:]
            mine = jnp.where(core == 0, first, second)
            partners = jnp.where(core == 0, second, first)
            return (mine + swap(partners.astype(bf16)).astype(f32)).T

    def gather(own):
        along = list(own)
        pieces, others = [list(along)], []
        for step in range(1, chips):
            along = [move(part, lambda y: y >= step - 1) for part in along]
            pieces.append(list(along))
            others.append([swap(part) for part in along])
        return pieces, others

    def assemble(pieces, others, after=()):
        parts = []
        for j, first in enumerate(pieces[0]):
            shards = [first]
            for p in range(1, chips):
                here, there = pieces[p][j], others[chips - p - 1][j]
                shards.append(jnp.where(position >= p, here, there))
            parts.append(jnp.concatenate(shards, axis=0))
        return fence(order, *parts, after=after)

    first_own, second_own = value_weight[0], output_weight[0]
    first_partner, second_partner = swap(first_own), swap(second_own)

    joined = join_cores(order, first_own, first_partner, HALVES, (second_partner,))
    pieces, others = gather(joined)
    last = pieces[-1]

    exponents = fence(order, delta_exponents, after=(pieces[2][1],))[0]
    bits = replicas.bit_length() - 1
    if replicas != 1 << bits or bits < 1:
        raise ValueError("replicas")
    rows_half = base_params.shape[0] // 2
    sums, early = [], []
    for index in range(2):
        rows = slice(index * rows_half, (index + 1) * rows_half)
        scale = jnp.exp2(exponents[0, rows].astype(f32))[:, None]
        total = delta_values[0, rows].astype(f32) * scale
        for turn in range(bits):
            mine = total.astype(bf16)
            bit = 1 << ((turn + index) % bits)
            theirs = lax.ppermute(mine, "replica", [(i, i ^ bit) for i in range(replicas)])
            if turn == 0:
                early.append(theirs)
            total = mine.astype(f32) + theirs.astype(f32)
        sums.append((mine, theirs))

    joined = join_cores(order, second_own, second_partner, 1, (last[0],))
    ahead = gather(joined)
    normed = in_places(order, tokens[0], norm_gain, chips, (*others[-1], *others[-2]))
    values = jnp.concatenate(
        [
            jnp.dot(normed, part, preferred_element_type=f32).astype(bf16)
            for part in assemble(pieces, others, (ahead[0][1][0],))
        ],
        axis=1,
    )
    cotangent = in_places(order, out_cotangent[0], None, chips)
    pieces, others = ahead
    values = fence(order, values, after=(pieces[1][0], *early))[0]
    first = Gradient(values, cotangent, (pieces[2][0],))
    sent = [first.reduce(step) for step in range(1, chips)]

    weight = assemble(pieces, others, ())[0]
    mid = jnp.dot(cotangent, weight, preferred_element_type=f32).astype(bf16)
    mid = fence(order, mid, after=(sent[-1],))[0]
    half = mid.shape[1] // HALVES
    second = []
    for j in range(HALVES):
        after = (first.arrived,) if j else ()
        second.append(Gradient(mid[:, j * half : (j + 1) * half], normed, after))
    for step in range(1, chips):
        sent = tuple(gradient.reduce(step) for gradient in second)
        if step == 1:
            theirs = fence(order, *(pair[1] for pair in sums), after=sent)
    output_grad = first.finish()

    total = [a.astype(f32) + b.astype(f32) for (a, _), b in zip(sums, theirs)]
    delta = jnp.concatenate(total) * (1.0 / replicas)
    new_base, new_momentum = nesterov(delta, base_params, outer_momentum)
    value_grad = jnp.concatenate([gradient.finish() for gradient in second], axis=1)
    return (value_grad[None], output_grad[None], new_base, new_momentum)


def solution(mesh):
    return jax.shard_map(
        per_device,
        mesh=mesh,
        in_specs=(
            P("replica", "fsdp", None),
            P(),
            P("replica", "fsdp", None),
            P("replica", "fsdp", None),
            P("replica", "fsdp", None),
            P("fsdp", None),
            P("fsdp", None),
            P("replica", "fsdp", None),
            P("replica", "fsdp"),
        ),
        out_specs=(
            P("replica", "fsdp", None),
            P("replica", "fsdp", None),
            P("fsdp", None),
            P("fsdp", None),
        ),
        check_vma=False,
    )
```

```python
import jax
import jax.numpy as jnp
from jax import lax
from jax.experimental import pallas as pl
from jax.experimental.pallas import tpu as pltpu
from jax.sharding import PartitionSpec as P

HALVES = 2
ROW_TILE = 128
FLOPS_PER_US = 10**9
ANY = pl.BlockSpec(memory_space=pl.ANY)


def move_perm(chips, active):
    pairs = []
    for z in range(chips):
        if z < chips - 1 and active(z):
            pairs.append((2 * z, 2 * z + 2))
        if z > 0 and active(chips - 1 - z):
            pairs.append((2 * z + 1, 2 * z - 1))
    return pairs


class Order:
    def __init__(self, place):
        self.place = place
        self.last = ()

    def __call__(
        self, kernel, args, in_specs, out_shape, scratch, vmem, after=(), aliases=None, grid=1,
        out_specs=None, us=1.0,
    ):
        after = self.last + tuple(after)
        count = len(args)

        def ordered(place_ref, *refs):
            kernel(place_ref, *refs[:count], *refs[count + len(after) :])

        result = pl.pallas_call(
            ordered,
            grid_spec=pltpu.PrefetchScalarGridSpec(
                num_scalar_prefetch=1,
                grid=(grid,),
                in_specs=in_specs + [ANY] * len(after),
                out_specs=out_specs or [ANY] * len(out_shape),
                scratch_shapes=scratch,
            ),
            out_shape=out_shape,
            input_output_aliases={1 + i: o for i, o in (aliases or {}).items()},
            compiler_params=pltpu.CompilerParams(vmem_limit_bytes=vmem * 1024 * 1024),
            cost_estimate=pl.CostEstimate(flops=int(us * FLOPS_PER_US), bytes_accessed=1, transcendentals=0),
            name=kernel.__qualname__.split(".")[0],
        )(self.place, *args, *after)
        self.last = (result[0],)
        return result


def copies(pairs, sems):
    started = [pltpu.make_async_copy(a, b, sems.at[i]) for i, (a, b) in enumerate(pairs)]
    for copy in started:
        copy.start()
    return started


def fence(order, *values, after=()):
    def fence(*refs):
        pass

    shapes = [jax.ShapeDtypeStruct(v.shape, v.dtype) for v in values]
    aliases = {i: i for i in range(len(values))}
    return order(fence, values, [ANY] * len(values), shapes, [], 4, after, aliases)


def in_places(order, x, gain, chips, after=()):
    rows, model = x.shape
    block = model // chips

    def run(place_ref, x_ref, *refs):
        out_ref = refs[-1]
        if gain is not None:
            xf = x_ref[...].astype(jnp.float32)
            scale = lax.rsqrt(jnp.mean(xf * xf, axis=1, keepdims=True) + 1e-05)
        for p in range(chips):
            cols = pl.ds(pl.multiple_of(place_ref[p] * block, block), block)
            part = x_ref[:, cols]
            if gain is not None:
                part = part.astype(jnp.float32) * scale * refs[0][:, cols]
            out_ref[:, p * block : (p + 1) * block] = part.astype(jnp.bfloat16)

    tile = pl.BlockSpec((ROW_TILE, model), lambda i, _: (i, 0))
    gains = () if gain is None else (gain[None],)
    return order(
        run,
        (x, *gains),
        [tile] + [pl.BlockSpec((1, model), lambda i, _: (0, 0))] * len(gains),
        [jax.ShapeDtypeStruct((rows, model), jnp.bfloat16)],
        [],
        16,
        after,
        grid=rows // ROW_TILE,
        out_specs=[tile],
        us=5.0,
    )[0]


def join_cores(order, own, partner, parts, after=()):
    rows, features = own.shape
    piece = features // parts

    def run(place_ref, own_ref, partner_ref, *refs):
        out_refs, sems = refs[:parts], refs[parts]
        core = place_ref[place_ref.shape[0] - 1]
        pairs = []
        for j, out_ref in enumerate(out_refs):
            cols = pl.ds(j * piece, piece)
            for source, where in ((own_ref, core), (partner_ref, 1 - core)):
                target = out_ref.at[pl.ds(pl.multiple_of(where * rows, rows), rows)]
                pairs.append((source.at[:, cols], target))
        for copy in copies(pairs, sems):
            copy.wait()

    return order(
        run,
        (own, partner),
        [ANY, ANY],
        [jax.ShapeDtypeStruct((2 * rows, piece), jnp.bfloat16)] * parts,
        [pltpu.SemaphoreType.DMA((2 * parts,))],
        4,
        after,
    )


def nesterov(delta, base_part, momentum_part):
    momentum_next = 0.9 * momentum_part + delta
    base_next = (base_part.astype(jnp.float32) - 0.7 * (delta + 0.9 * momentum_next)).astype(
        jnp.bfloat16
    )
    return (base_next, momentum_next)


def per_device(
    tokens,
    norm_gain,
    value_weight,
    output_weight,
    out_cotangent,
    base_params,
    outer_momentum,
    delta_values,
    delta_exponents,
):
    replicas = lax.axis_size("replica")
    devices = lax.axis_size("fsdp")
    chips = devices // 2
    me = lax.axis_index("fsdp")
    chip, core = me // 2, me % 2
    position = chip + core * (chips - 1 - 2 * chip)
    way = 1 - 2 * core
    behind = [(chip - way * s + chips) % chips for s in range(chips)]
    order = Order(jnp.stack([*behind, position, core]).astype(jnp.int32))
    shard = value_weight.shape[1]
    block = 2 * shard
    bf16, f32 = jnp.bfloat16, jnp.float32

    def swap(value):
        return lax.ppermute(value, "fsdp", [(i, i ^ 1) for i in range(devices)])

    def move(value, active=lambda y: True):
        return lax.ppermute(value, "fsdp", move_perm(chips, active))

    class Gradient:
        def __init__(self, mid, x, after=(), late=()):
            terms = lax.dot_general(mid, x, (((0,), (0,)), ((), ())), preferred_element_type=f32)
            self.terms = terms.astype(bf16)
            if after:
                self.terms = fence(order, self.terms, after=after)[0]
            self.across = [None] + [swap(self.block(chips - s)) for s in range(1, chips)]
            self.arrived = None
            if late:
                self.across[1] = fence(order, self.across[1], after=late)[0]

        def block(self, place):
            return self.terms[:, place * block : (place + 1) * block]

        def message(self, step):
            term = self.block(step).astype(f32) + self.across[step].astype(f32)
            if self.arrived is not None:
                term = term + self.arrived.astype(f32)
            return term.astype(bf16)

        def reduce(self, step):
            message = self.message(step)
            self.arrived = move(message, lambda y: y <= step - 1)
            return message

        def finish(self):
            whole = self.block(0).astype(f32) + self.arrived.astype(f32)
            first, second = whole[:, :shard], whole[:, shard:]
            mine = jnp.where(core == 0, first, second)
            partners = jnp.where(core == 0, second, first)
            return (mine + swap(partners.astype(bf16)).astype(f32)).T

    def gather(own):
        along = list(own)
        pieces, others = [list(along)], []
        for step in range(1, chips):
            along = [move(part, lambda y: y >= step - 1) for part in along]
            pieces.append(list(along))
            others.append([swap(part) for part in along])
        return pieces, others

    def assemble(pieces, others, after=()):
        parts = []
        for j, first in enumerate(pieces[0]):
            shards = [first]
            for p in range(1, chips):
                here, there = pieces[p][j], others[chips - p - 1][j]
                shards.append(jnp.where(position >= p, here, there))
            parts.append(jnp.concatenate(shards, axis=0))
        return fence(order, *parts, after=after)

    first_own, second_own = value_weight[0], output_weight[0]
    first_partner, second_partner = swap(first_own), swap(second_own)

    joined = join_cores(order, first_own, first_partner, HALVES, (second_partner,))
    pieces, others = gather(joined)
    last = pieces[-1]

    exponents = fence(order, delta_exponents, after=(pieces[-1][1],))[0]
    bits = replicas.bit_length() - 1
    if replicas != 1 << bits or bits < 1:
        raise ValueError("replicas")
    rows_half = base_params.shape[0] // 2
    sums, early = [], []
    for index in range(2):
        rows = slice(index * rows_half, (index + 1) * rows_half)
        scale = jnp.exp2(exponents[0, rows].astype(f32))[:, None]
        total = delta_values[0, rows].astype(f32) * scale
        for turn in range(bits):
            mine = total.astype(bf16)
            bit = 1 << ((turn + index) % bits)
            theirs = lax.ppermute(mine, "replica", [(i, i ^ bit) for i in range(replicas)])
            if turn == 0:
                early.append(theirs)
            total = mine.astype(f32) + theirs.astype(f32)
        sums.append((mine, theirs))

    joined = join_cores(order, second_own, second_partner, 1, (last[0],))
    ahead = gather(joined)
    normed = in_places(order, tokens[0], norm_gain, chips, (*others[-1], *others[-2]))
    values = jnp.concatenate(
        [
            jnp.dot(normed, part, preferred_element_type=f32).astype(bf16)
            for part in assemble(pieces, others, (ahead[0][1][0],))
        ],
        axis=1,
    )
    cotangent = in_places(order, out_cotangent[0], None, chips)
    pieces, others = ahead
    values = fence(order, values, after=(pieces[1][0], *early))[0]
    first = Gradient(values, cotangent, (pieces[2][0],))
    sent = [first.reduce(step) for step in range(1, chips)]

    weight = assemble(pieces, others)[0]
    mid = jnp.dot(cotangent, weight, preferred_element_type=f32).astype(bf16)
    mid = fence(order, mid, after=(sent[-1],))[0]
    half = mid.shape[1] // HALVES
    second = []
    for j in range(HALVES):
        late = () if j else ()
        second.append(Gradient(mid[:, j * half : (j + 1) * half], normed, (), late))
    for step in range(1, chips):
        sent = tuple(gradient.reduce(step) for gradient in second)
        if step == 1:
            theirs = fence(order, *(pair[1] for pair in sums), after=sent)
    output_grad = first.finish()

    total = [a.astype(f32) + b.astype(f32) for (a, _), b in zip(sums, theirs)]
    delta = jnp.concatenate(total) * (1.0 / replicas)
    new_base, new_momentum = nesterov(delta, base_params, outer_momentum)
    value_grad = jnp.concatenate([gradient.finish() for gradient in second], axis=1)
    return (value_grad[None], output_grad[None], new_base, new_momentum)


def solution(mesh):
    return jax.shard_map(
        per_device,
        mesh=mesh,
        in_specs=(
            P("replica", "fsdp", None),
            P(),
            P("replica", "fsdp", None),
            P("replica", "fsdp", None),
            P("replica", "fsdp", None),
            P("fsdp", None),
            P("fsdp", None),
            P("replica", "fsdp", None),
            P("replica", "fsdp"),
        ),
        out_specs=(
            P("replica", "fsdp", None),
            P("replica", "fsdp", None),
            P("fsdp", None),
            P("fsdp", None),
        ),
        check_vma=False,
    )
```
